32 devices in a mesh: gx: 2 (over x), gy: 16 (over z, y, core).
Axes of the slice: x: 2, y: 2, z: 4, core: 2. Of those that a mesh axis runs over, the one named last changes fastest.
Arguments:
- node_feats: bfloat16 [8192, 512], P(('gx', 'gy')), may hold values from -6 to 6
- grad_out: bfloat16 [8192, 512], P(('gx', 'gy')), may hold values from -6 to 6
- log_sum_exp: float32 [8, 8192], P(None, ('gx', 'gy')), may hold values from 7.5 to 9
- w_query: bfloat16 [512, 512], replicated, may hold values from -0.25 to 0.25
- w_key: bfloat16 [512, 512], replicated, may hold values from -0.25 to 0.25
- w_value: bfloat16 [512, 512], replicated, may hold values from -0.25 to 0.25
- w_output: bfloat16 [512, 512], replicated, may hold values from -0.25 to 0.25
- partners: int32 [32, 3], replicated, may hold values from 0 to 31, as said below
Outputs:
- grad_nodes: bfloat16 [8192, 512], P(('gx', 'gy'))
- weight_grads: float32 [512, 2048], P('gx', 'gy')
The draws below stay inside these ranges and needn't reach their ends.
Inputs may be any that keep to these rules, and one draw needn't show every extreme that they name: Row b holds three different blocks, none of them b, and partners[partners[b, j], j] = b for each column j: each column is a perfect matching of the 32 blocks.
All inputs are finite; a program needn't handle non-finite values.
Results may differ from the reference program's by a relative error of at most 0.019.
Values may be sent and summed in bfloat16 or wider, within the bound.
No kernel may reach another device: no remote copies, remote signals or barrier semaphores. Data moves between devices by JAX's collectives and lax.ppermute only.
A program may use at most 64 MiB of HBM per device.

```python
import jax
import jax.numpy as jnp
from jax import lax

D = 512
H = 8
HD = 64
BLOCK = 256
NB = 32
NODES = 8192


def draw_partners(key, part):
    first, second = jax.random.split(jax.random.fold_in(key, 11))
    order = jax.random.permutation(first, NB).astype(jnp.int32)
    masks = (jax.random.permutation(second, NB - 1)[:3] + 1).astype(jnp.int32)
    inverse = jnp.argsort(order).astype(jnp.int32)
    spots = jnp.bitwise_xor(inverse[:, None], masks[None, :])
    return order[spots].astype(jnp.int32)


def spiked(values, key, source, target, shards_of, factor):
    owner, partner = [(jnp.arange(values.shape[position]) // (values.shape[position] // shards_of)).reshape([-1 if axis == position else 1 for axis in range(values.ndim)]) for position in (source, target)]
    chosen = jax.random.permutation(key, shards_of)[partner]
    strong = (owner == chosen) | (owner == (partner + shards_of // 2) % shards_of)
    return jnp.where(strong, factor * values, values)


def level_of(stream_key, extent, pieces, low, high):
    gain = 1.0
    for position, shards_of in pieces:
        draws = jax.random.uniform(jax.random.fold_in(jax.random.fold_in(stream_key, 6), position), (shards_of,), jnp.float32, low / len(pieces), high / len(pieces))
        gain = gain * jnp.repeat(jnp.exp(draws), extent[position] // shards_of).reshape((-1,) + (1,) * (len(extent) - 1 - position))
    return gain


def noise(stream_key, dims, scale, bound, cuts=(), kind=jnp.bfloat16):
    drawn = jax.random.normal(stream_key, dims, jnp.float32) * scale
    if len(cuts) > 0:
        drawn = level_of(stream_key, dims, cuts, -0.22, 0.18) * drawn
    return jnp.clip(drawn, min=-bound, max=bound).astype(kind)


def gaussian_with(key, extent, width, most, pieces, heavy, held_as=jnp.bfloat16):
    result = width * jax.random.normal(key, extent, jnp.float32)
    if pieces:
        result = result * level_of(key, extent, pieces, -0.22, 0.18)
    return jnp.clip(spiked(result, jax.random.fold_in(key, 3), *heavy), -most, most).astype(held_as)


def setup_inputs(seed: int = 0) -> dict:
    key_of = jax.random.split(jax.random.key(seed), 9)
    return {
        "node_feats": gaussian_with(key_of[0], (NODES, D), 1.0, 6.0, ((0, 32),), (0, 1, 32, 2.75)),
        "grad_out": gaussian_with(key_of[1], (NODES, D), 1.0, 6.0, ((0, 32),), (0, 1, 32, 2.75)),
        "log_sum_exp": jnp.clip(7.5 + 1.5 * jax.random.uniform(key_of[2], (H, NODES), jnp.float32) ** level_of(key_of[2], (H, NODES), ((1, 32),), -0.2, 0.2), 7.5, 9.0),
        "w_query": noise(key_of[3], (D, D), D ** -0.5, 0.25),
        "w_key": noise(key_of[4], (D, D), D ** -0.5, 0.25),
        "w_value": noise(key_of[5], (D, D), D ** -0.5, 0.25),
        "w_output": noise(key_of[6], (D, D), D ** -0.5, 0.25),
        "partners": draw_partners(jax.random.fold_in(key_of[8], 71), 0),
    }


def block_terms(query_blk, key_rows, value_rows, dout_blk, lse_blk):
    scaling = HD ** -0.5
    query_f = query_blk.astype(jnp.float32).reshape(BLOCK, H, HD)
    key_f = key_rows.astype(jnp.float32).reshape(4 * BLOCK, H, HD)
    value_f = value_rows.astype(jnp.float32).reshape(4 * BLOCK, H, HD)
    dout_f = dout_blk.astype(jnp.float32).reshape(BLOCK, H, HD)
    scores = jnp.einsum('ihe,jhe->hij', query_f, key_f) * scaling
    probs = jnp.exp(jnp.minimum(scores - lse_blk[:, :, None], 0.0))
    probs_low = probs.astype(jnp.bfloat16)
    probs_back = probs_low.astype(jnp.float32)
    out_blk = jnp.einsum('hij,jhe->ihe', probs_back, value_f).reshape(BLOCK, D).astype(jnp.bfloat16)
    row_delta = jnp.sum(dout_f * out_blk.astype(jnp.float32).reshape(BLOCK, H, HD), axis=-1).T
    grad_probs = jnp.einsum('ihe,jhe->hij', dout_f, value_f)
    grad_scores = (probs * (grad_probs - row_delta[:, :, None]) * scaling).astype(jnp.bfloat16)
    grad_float = grad_scores.astype(jnp.float32)
    grad_q = jnp.einsum('hij,jhe->ihe', grad_float, key_f).reshape(BLOCK, D).astype(jnp.bfloat16)
    grad_k = jnp.einsum('hij,ihe->jhe', grad_float, query_f).reshape(4, BLOCK, D)
    grad_v = jnp.einsum('hij,ihe->jhe', probs_back, dout_f).reshape(4, BLOCK, D)
    return grad_q, out_blk, grad_k, grad_v


def reference(node_feats, grad_out, log_sum_exp, w_query, w_key, w_value, w_output, partners):
    query = jnp.dot(node_feats, w_query, preferred_element_type=jnp.float32).astype(jnp.bfloat16)
    key_all = jnp.dot(node_feats, w_key, preferred_element_type=jnp.float32).astype(jnp.bfloat16)
    value_all = jnp.dot(node_feats, w_value, preferred_element_type=jnp.float32).astype(jnp.bfloat16)
    d_out = jnp.dot(grad_out, w_output.T, preferred_element_type=jnp.float32).astype(jnp.bfloat16)
    query_blocks = query.reshape(NB, BLOCK, D)
    key_blocks = key_all.reshape(NB, BLOCK, D)
    value_blocks = value_all.reshape(NB, BLOCK, D)
    dout_blocks = d_out.reshape(NB, BLOCK, D)
    lse_blocks = log_sum_exp.reshape(H, NB, BLOCK).transpose(1, 0, 2)

    def step(carry, index):
        acc_key, acc_value = carry
        members = jnp.concatenate([index[None], partners[index]]).astype(jnp.int32)
        key_rows = key_blocks[members].reshape(4 * BLOCK, D)
        value_rows = value_blocks[members].reshape(4 * BLOCK, D)
        grad_q, out_blk, grad_k, grad_v = block_terms(query_blocks[index], key_rows, value_rows, dout_blocks[index], lse_blocks[index])
        acc_key = acc_key.at[members].add(grad_k)
        acc_value = acc_value.at[members].add(grad_v)
        return (acc_key, acc_value), (grad_q, out_blk)

    start = (jnp.zeros((NB, BLOCK, D), jnp.float32), jnp.zeros((NB, BLOCK, D), jnp.float32))
    (acc_key, acc_value), (grad_q, out_all) = lax.scan(step, start, jnp.arange(NB, dtype=jnp.int32))
    grad_query = grad_q.reshape(NODES, D)
    out_rows = out_all.reshape(NODES, D)
    grad_key = acc_key.reshape(NODES, D).astype(jnp.bfloat16)
    grad_value = acc_value.reshape(NODES, D).astype(jnp.bfloat16)
    weight_grads = jnp.concatenate([
        jnp.dot(node_feats.T, grad_query, preferred_element_type=jnp.float32),
        jnp.dot(node_feats.T, grad_key, preferred_element_type=jnp.float32),
        jnp.dot(node_feats.T, grad_value, preferred_element_type=jnp.float32),
        jnp.dot(out_rows.T, grad_out, preferred_element_type=jnp.float32)], axis=1)
    total = jnp.dot(grad_query, w_query.T, preferred_element_type=jnp.float32)
    total = total + jnp.dot(grad_key, w_key.T, preferred_element_type=jnp.float32)
    total = total + jnp.dot(grad_value, w_value.T, preferred_element_type=jnp.float32)
    return total.astype(jnp.bfloat16), weight_grads
```

```python
import functools
import math

import jax
import jax.numpy as jnp
from jax import lax
from jax.experimental import pallas as pl
from jax.experimental.pallas import tpu as pltpu
from jax.sharding import PartitionSpec as P

AXES = ("gx", "gy")
LOW = jnp.bfloat16
WIDE = jnp.float32


def dot(left, right):
    return jnp.dot(left, right, preferred_element_type=WIDE)


def dot_nt(left, right):
    return lax.dot_general(left, right, (((1,), (1,)), ((), ())), preferred_element_type=WIDE)


def exchange(pieces):
    return lax.all_to_all(pieces, AXES, split_axis=0, concat_axis=0, tiled=True)


def attention_kernel(
    head_size,
    group,
    far_ref,
    key_own_ref,
    value_own_ref,
    key_own_t_ref,
    value_own_t_ref,
    query_t_ref,
    d_out_t_ref,
    query_ref,
    d_out_ref,
    lse_ref,
    w_key_ref,
    w_value_ref,
    w_key_t_ref,
    w_value_t_ref,
    w_query_t_ref,
    terms_ref,
    own_ref,
    grad_query_t_ref,
    out_t_ref,
    grad_key_ref,
    grad_value_ref,
    key_ref,
    value_ref,
    key_t_ref,
    value_t_ref,
):
    heads = lse_ref.shape[0]
    block = query_ref.shape[0]
    scaling = head_size ** (-0.5)
    log2e = math.log2(math.e)
    far = far_ref[...]
    key_ref[:block] = key_own_ref[...]
    value_ref[:block] = value_own_ref[...]
    key_t_ref[:, :block] = key_own_t_ref[...]
    value_t_ref[:, :block] = value_own_t_ref[...]
    key_ref[block:] = dot(far, w_key_ref[...]).astype(LOW)
    value_ref[block:] = dot(far, w_value_ref[...]).astype(LOW)
    key_t_ref[:, block:] = dot_nt(w_key_t_ref[...], far).astype(LOW)
    value_t_ref[:, block:] = dot_nt(w_value_t_ref[...], far).astype(LOW)
    span = group * head_size
    for first in range(0, heads, group):
        cols = slice(first * head_size, first * head_size + span)
        key = key_ref[:, cols]
        value = value_ref[:, cols]
        row = lax.broadcasted_iota(jnp.int32, (span, block), 0) // head_size
        col = lax.broadcasted_iota(jnp.int32, (block, span), 1) // head_size
        query_t = query_t_ref[cols, :]
        d_out_t = d_out_t_ref[cols, :]
        query = query_ref[:, cols]
        d_out = d_out_ref[:, cols]
        zero_t = jnp.zeros_like(query_t)
        zero = jnp.zeros_like(query)
        grad_key = None
        grad_value = None
        for inner in range(group):
            head = first + inner
            rows = slice(head * head_size, (head + 1) * head_size)
            score = dot(key, jnp.where(row == inner, query_t, zero_t))
            shift = lse_ref[head : head + 1, :] * log2e
            prob = jnp.exp2(jnp.minimum(score * (scaling * log2e) - shift, 0.0))
            prob_low = prob.astype(LOW)
            out_t = dot(value_t_ref[rows, :], prob_low).astype(LOW)
            out_t_ref[rows, :] = out_t
            d_rows = d_out_t_ref[rows, :]
            delta = jnp.sum(d_rows.astype(WIDE) * out_t.astype(WIDE), axis=0, keepdims=True) * scaling
            grad_prob = dot(value, jnp.where(row == inner, d_out_t * scaling, zero_t))
            grad_score = (prob * (grad_prob - delta)).astype(LOW)
            grad_query_t_ref[rows, :] = dot(key_t_ref[rows, :], grad_score).astype(LOW)
            part_key = dot(grad_score, jnp.where(col == inner, query, zero))
            part_value = dot(prob_low, jnp.where(col == inner, d_out, zero))
            grad_key = part_key if grad_key is None else grad_key + part_key
            grad_value = part_value if grad_value is None else grad_value + part_value
        grad_key_ref[:, cols] = grad_key.astype(LOW)
        grad_value_ref[:, cols] = grad_value.astype(LOW)
    total = dot(grad_key_ref[...], w_key_t_ref[...]) + dot(grad_value_ref[...], w_value_t_ref[...])
    terms_ref[...] = total[block:].astype(LOW)
    own_ref[...] = total[:block] + lax.dot_general(
        grad_query_t_ref[...],
        w_query_t_ref[...],
        (((0,), (0,)), ((), ())),
        preferred_element_type=WIDE,
    )


def attention(head_size, block, width, heads, *operands):
    members = 4 * block
    group = max(1, 128 // head_size)
    return pl.pallas_call(
        functools.partial(attention_kernel, head_size, group),
        out_shape=(
            jax.ShapeDtypeStruct((3 * block, width), LOW),
            jax.ShapeDtypeStruct((block, width), WIDE),
            jax.ShapeDtypeStruct((width, block), LOW),
            jax.ShapeDtypeStruct((width, block), LOW),
            jax.ShapeDtypeStruct((members, width), LOW),
            jax.ShapeDtypeStruct((members, width), LOW),
        ),
        in_specs=[pl.BlockSpec(memory_space=pltpu.VMEM)] * len(operands),
        out_specs=(pl.BlockSpec(memory_space=pltpu.VMEM),) * 6,
        scratch_shapes=[
            pltpu.VMEM((members, width), LOW),
            pltpu.VMEM((members, width), LOW),
            pltpu.VMEM((width, members), LOW),
            pltpu.VMEM((width, members), LOW),
        ],
        compiler_params=pltpu.CompilerParams(vmem_limit_bytes=48 * 1024 * 1024),
        cost_estimate=pl.CostEstimate(
            flops=12 * block * members * width + 8 * members * width * width,
            bytes_accessed=16 * members * width,
            transcendentals=heads * block * members,
        ),
    )(*operands)


def bits_of(count):
    return [1 << position for position in range(count.bit_length() - 1)]


def halve(parts, axis, mask, me, devices):
    mine = jnp.where((me & mask) != 0, 1, 0)
    send = lax.dynamic_index_in_dim(parts, 1 - mine, axis, keepdims=False)
    keep = lax.dynamic_index_in_dim(parts, mine, axis, keepdims=False)
    got = lax.ppermute(send, AXES, [(device, device ^ mask) for device in range(devices)])
    return (keep.astype(WIDE) + got.astype(WIDE)).astype(LOW)


def scatter_sum(partial):
    n_outer = lax.axis_size("gx")
    n_inner = lax.axis_size("gy")
    devices = n_outer * n_inner
    me = lax.axis_index("gx") * n_inner + lax.axis_index("gy")
    rows, cols = partial.shape
    outer = [mask * n_inner for mask in bits_of(n_outer)]
    inner = bits_of(n_inner)
    blocks = partial.reshape(n_outer, rows // n_outer, n_inner, cols // n_inner)
    blocks = blocks.transpose(0, 2, 1, 3)
    high_first = outer[::-1] + inner[::-1]
    half = rows // n_outer // 2
    orders = (
        inner[:1] + outer + inner[1:2] + inner[2:],
        inner[:1] + inner[1:2] + outer + inner[2:],
    )
    results = []
    for part, order in enumerate(orders):
        piece = blocks[:, :, part * half : (part + 1) * half]
        piece = piece.reshape((2,) * len(high_first) + (half, cols // n_inner))
        left = list(high_first)
        for mask in order:
            piece = halve(piece, left.index(mask), mask, me, devices)
            left.remove(mask)
        results.append(piece)
    return jnp.concatenate(results, axis=0).astype(WIDE)


def on_device(node_feats, grad_out, log_sum_exp, w_query, w_key, w_value, w_output, partners):
    block, width = node_feats.shape
    heads = log_sum_exp.shape[0]
    head_size = width // heads
    devices = partners.shape[0]
    piece = block // devices
    spread = exchange(node_feats.reshape(devices, piece, width))
    chosen = spread[partners]
    arrived = exchange(chosen)
    far = arrived.transpose(1, 0, 2, 3).reshape(3 * block, width)

    w_query_t, w_key_t, w_value_t = w_query.T, w_key.T, w_value.T
    query = dot(node_feats, w_query).astype(LOW)
    query_t = dot_nt(w_query_t, node_feats).astype(LOW)
    key_own = dot(node_feats, w_key).astype(LOW)
    key_own_t = dot_nt(w_key_t, node_feats).astype(LOW)
    value_own = dot(node_feats, w_value).astype(LOW)
    value_own_t = dot_nt(w_value_t, node_feats).astype(LOW)
    d_out = dot_nt(grad_out, w_output).astype(LOW)
    d_out_t = dot_nt(w_output, grad_out).astype(LOW)

    terms, own, grad_query_t, out_t, grad_key, grad_value = attention(
        head_size,
        block,
        width,
        heads,
        far,
        key_own,
        value_own,
        key_own_t,
        value_own_t,
        query_t,
        d_out_t,
        query,
        d_out,
        log_sum_exp,
        w_key,
        w_value,
        w_key_t,
        w_value_t,
        w_query_t,
    )

    returned = exchange(terms.reshape(3, devices, piece, width).transpose(1, 0, 2, 3))
    summed = sum(returned[partners[:, match], match].astype(WIDE) for match in range(3))
    back = exchange(summed.astype(LOW)).reshape(block, width)
    grad_nodes = (own + back.astype(WIDE)).astype(LOW)

    feats_all = jnp.concatenate([node_feats, far], axis=0)
    partial = jnp.concatenate(
        [
            dot_nt(node_feats.T, grad_query_t),
            dot(feats_all.T, grad_key),
            dot(feats_all.T, grad_value),
            dot(out_t, grad_out),
        ],
        axis=1,
    ).astype(LOW)
    return grad_nodes, scatter_sum(partial)


def solution(mesh):
    return jax.shard_map(
        on_device,
        mesh=mesh,
        in_specs=(
            P(AXES, None),
            P(AXES, None),
            P(None, AXES),
            P(),
            P(),
            P(),
            P(),
            P(),
        ),
        out_specs=(P(AXES, None), P("gx", "gy")),
        check_vma=False,
    )
```

```python
import functools
import math

import jax
import jax.numpy as jnp
from jax import lax
from jax.experimental import pallas as pl
from jax.experimental.pallas import tpu as pltpu
from jax.sharding import PartitionSpec as P

AXES = ("gx", "gy")
LOW = jnp.bfloat16
WIDE = jnp.float32


def dot(left, right):
    return jnp.dot(left, right, preferred_element_type=WIDE)


def dot_nt(left, right):
    return lax.dot_general(left, right, (((1,), (1,)), ((), ())), preferred_element_type=WIDE)


def exchange(pieces):
    return lax.all_to_all(pieces, AXES, split_axis=0, concat_axis=0, tiled=True)


VMEM = pl.BlockSpec(memory_space=pltpu.VMEM)
ANY = pl.BlockSpec(memory_space=pl.ANY)
FULL_VMEM = 56 * 1024 * 1024


def shaped(shape, dtype=LOW):
    return jax.ShapeDtypeStruct(shape, dtype)


def project_kernel(
    feats_ref,
    grad_out_ref,
    w_query_ref,
    w_key_ref,
    w_value_ref,
    w_output_ref,
    query_ref,
    query_t_ref,
    d_out_ref,
    d_out_t_ref,
    key_ref,
    key_t_ref,
    value_ref,
    value_t_ref,
    w_query_t_ref,
    w_key_t_ref,
    w_value_t_ref,
    feats_t_ref,
):
    feats = feats_ref[...]
    feats_t_ref[...] = feats.T
    for w_ref, w_t_ref, plain_ref, turned_ref in (
        (w_query_ref, w_query_t_ref, query_ref, query_t_ref),
        (w_key_ref, w_key_t_ref, key_ref, key_t_ref),
        (w_value_ref, w_value_t_ref, value_ref, value_t_ref),
    ):
        w_t = w_ref[...].T
        w_t_ref[...] = w_t
        plain_ref[...] = dot(feats, w_ref[...]).astype(LOW)
        turned_ref[...] = dot_nt(w_t, feats).astype(LOW)
    d_out_ref[...] = dot_nt(grad_out_ref[...], w_output_ref[...]).astype(LOW)
    d_out_t_ref[...] = dot_nt(w_output_ref[...], grad_out_ref[...]).astype(LOW)


def project(node_feats, grad_out, *weights):
    block, width = node_feats.shape
    plain, turned, square = shaped((block, width)), shaped((width, block)), shaped((width, width))
    return pl.pallas_call(
        project_kernel,
        out_shape=(plain, turned) * 4 + (square,) * 3 + (turned,),
        in_specs=[VMEM] * 6,
        out_specs=(VMEM,) * 12,
        compiler_params=pltpu.CompilerParams(vmem_limit_bytes=FULL_VMEM),
        cost_estimate=pl.CostEstimate(
            flops=16 * block * width * width,
            bytes_accessed=2 * (10 * block * width + 7 * width * width),
            transcendentals=0,
        ),
    )(node_feats, grad_out, *weights)


def attention_kernel(
    head_size,
    group,
    stages,
    n_inner,
    me_ref,
    lse_ref,
    arrived_hbm,
    query_hbm,
    query_t_hbm,
    d_out_hbm,
    d_out_t_hbm,
    key_own_hbm,
    key_own_t_hbm,
    value_own_hbm,
    value_own_t_hbm,
    w_query_t_hbm,
    w_key_t_hbm,
    w_value_t_hbm,
    feats_t_hbm,
    grad_out_hbm,
    terms_hbm,
    own_hbm,
    keep_hbm,
    send_hbm,
    arrived_ref,
    query_ref,
    query_t_ref,
    d_out_ref,
    d_out_t_ref,
    w_query_t_ref,
    w_key_t_ref,
    w_value_t_ref,
    feats_t_ref,
    grad_out_ref,
    key_ref,
    value_ref,
    key_t_ref,
    value_t_ref,
    terms_ref,
    own_ref,
    grad_query_t_ref,
    out_t_ref,
    grad_key_ref,
    grad_value_ref,
    keep_ref,
    send_ref,
    in_sem,
    out_sem,
):
    heads = lse_ref.shape[0]
    block, width = query_ref.shape
    scaling = head_size ** (-0.5)
    log2e = math.log2(math.e)

    def by_match(ref, match):
        return ref.at[:, match] if len(ref.shape) == 4 else ref.at[match]

    loads = []

    def load(source, target):
        copy = pltpu.make_async_copy(source, target, in_sem.at[len(loads)])
        copy.start()
        loads.append(copy)
        return copy

    stores = []

    def store(source, target):
        copy = pltpu.make_async_copy(source, target, out_sem.at[len(stores)])
        copy.start()
        stores.append(copy)

    first_need = load(by_match(arrived_hbm, 0), arrived_ref.at[0])
    key_need = load(w_key_t_hbm, w_key_t_ref)
    value_need = load(w_value_t_hbm, w_value_t_ref)
    far_needs = [load(by_match(arrived_hbm, match), arrived_ref.at[match]) for match in (1, 2)]
    own = pl.ds(0, block)
    head_needs = [
        load(key_own_hbm, key_ref.at[own]),
        load(value_own_hbm, value_ref.at[own]),
        load(key_own_t_hbm, key_t_ref.at[:, own]),
        load(value_own_t_hbm, value_t_ref.at[:, own]),
        load(query_t_hbm, query_t_ref),
        load(d_out_t_hbm, d_out_t_ref),
        load(query_hbm, query_ref),
        load(d_out_hbm, d_out_ref),
    ]
    last_needs = [
        load(w_query_t_hbm, w_query_t_ref),
        load(feats_t_hbm, feats_t_ref),
        load(grad_out_hbm, grad_out_ref),
    ]
    first_need.wait()
    key_need.wait()
    for match in range(3):
        here = slice((match + 1) * block, (match + 2) * block)
        if match > 0:
            far_needs[match - 1].wait()
        far = arrived_ref[match].reshape(block, width)
        key_ref[here] = dot_nt(far, w_key_t_ref[...]).astype(LOW)
        key_t_ref[:, here] = dot_nt(w_key_t_ref[...], far).astype(LOW)
        if match == 0:
            value_need.wait()
        value_ref[here] = dot_nt(far, w_value_t_ref[...]).astype(LOW)
        value_t_ref[:, here] = dot_nt(w_value_t_ref[...], far).astype(LOW)
    for copy in head_needs:
        copy.wait()
    span = group * head_size
    for first in range(0, heads, group):
        cols = slice(first * head_size, first * head_size + span)
        key = key_ref[:, cols]
        value = value_ref[:, cols]
        row = lax.broadcasted_iota(jnp.int32, (span, block), 0) // head_size
        col = lax.broadcasted_iota(jnp.int32, (block, span), 1) // head_size
        query_t = query_t_ref[cols, :]
        d_out_t = d_out_t_ref[cols, :]
        query = query_ref[:, cols]
        d_out = d_out_ref[:, cols]
        zero_t = jnp.zeros_like(query_t)
        zero = jnp.zeros_like(query)
        grad_key = None
        grad_value = None
        for inner in range(group):
            head = first + inner
            rows = slice(head * head_size, (head + 1) * head_size)
            score = dot(key, jnp.where(row == inner, query_t, zero_t))
            shift = lse_ref[head : head + 1, :] * log2e
            prob = jnp.exp2(jnp.minimum(score * (scaling * log2e) - shift, 0.0))
            prob_low = prob.astype(LOW)
            out_t = dot(value_t_ref[rows, :], prob_low).astype(LOW)
            out_t_ref[rows, :] = out_t
            d_rows = d_out_t_ref[rows, :]
            delta = jnp.sum(d_rows.astype(WIDE) * out_t.astype(WIDE), axis=0, keepdims=True) * scaling
            grad_prob = dot(value, jnp.where(row == inner, d_out_t * scaling, zero_t))
            grad_score = (prob * (grad_prob - delta)).astype(LOW)
            grad_query_t_ref[rows, :] = dot(key_t_ref[rows, :], grad_score).astype(LOW)
            part_key = dot(grad_score, jnp.where(col == inner, query, zero))
            part_value = dot(prob_low, jnp.where(col == inner, d_out, zero))
            grad_key = part_key if grad_key is None else grad_key + part_key
            grad_value = part_value if grad_value is None else grad_value + part_value
        grad_key_ref[:, cols] = grad_key.astype(LOW)
        grad_value_ref[:, cols] = grad_value.astype(LOW)
    for copy in last_needs:
        copy.wait()

    _, rows, cols = keep_ref.shape
    n_outer = width // rows
    me = me_ref[0]
    odd = me % 2 == 1

    def place(matrix, total):
        low = total.astype(LOW)
        for start in range(0, width, 2 * cols):
            inner = (matrix * width + start) // cols
            for outer in range(n_outer):
                differ = me ^ (outer * n_inner + inner)
                slot = 0
                for masks in stages:
                    for mask in masks:
                        slot = slot * 2 + jnp.where((differ & mask) != 0, 1, 0)
                here = slice(outer * rows, (outer + 1) * rows)
                left = low[here, start : start + cols]
                right = low[here, start + cols : start + 2 * cols]
                keep_ref[slot] = jnp.where(odd, right, left)
                send_ref[slot] = jnp.where(odd, left, right)

    feats_t = feats_t_ref[...]
    far_t = [arrived_ref[match].reshape(block, width).T for match in range(3)]
    place(3, dot(out_t_ref[...], grad_out_ref[...]))
    place(0, dot_nt(feats_t, grad_query_t_ref[...]))
    for matrix, ref in ((1, grad_key_ref), (2, grad_value_ref)):
        total = dot(feats_t, ref[:block])
        for match in range(3):
            total = total + dot(far_t[match], ref[(match + 1) * block : (match + 2) * block])
        place(matrix, total)
    store(send_ref, send_hbm)
    store(keep_ref, keep_hbm)
    for member in range(4):
        here = slice(member * block, (member + 1) * block)
        total = dot(grad_key_ref[here], w_key_t_ref[...])
        total = total + dot(grad_value_ref[here], w_value_t_ref[...])
        if member == 0:
            own_ref[...] = total + lax.dot_general(
                grad_query_t_ref[...],
                w_query_t_ref[...],
                (((0,), (0,)), ((), ())),
                preferred_element_type=WIDE,
            )
            store(own_ref, own_hbm)
        else:
            terms_ref[member - 1] = total.astype(LOW).reshape(terms_ref.shape[1:])
            store(terms_ref.at[member - 1], by_match(terms_hbm, member - 1))
    for copy in stores:
        copy.wait()


def attention(me, stages, arrived, projections, grad_out, log_sum_exp):
    n_outer, n_inner = lax.axis_size("gx"), lax.axis_size("gy")
    block, width = grad_out.shape
    heads = log_sum_exp.shape[0]
    head_size = width // heads
    members = 4 * block
    group = max(1, 128 // head_size)
    devices, _, piece, _ = arrived.shape
    whole_tiles = piece % 8 == 0
    if not whole_tiles:
        arrived = arrived.transpose(1, 0, 2, 3).reshape(3, block, width)
    staged = (3, devices, piece, width) if whole_tiles else (3, block, width)
    half = (devices // 2, width // n_outer, 4 * width // n_inner)
    plain, turned, square = (
        pltpu.VMEM((block, width), LOW),
        pltpu.VMEM((width, block), LOW),
        pltpu.VMEM((width, width), LOW),
    )
    long, long_t = pltpu.VMEM((members, width), LOW), pltpu.VMEM((width, members), LOW)
    terms, own, keep, send = pl.pallas_call(
        functools.partial(attention_kernel, head_size, group, stages, n_inner),
        out_shape=(shaped(arrived.shape), shaped((block, width), WIDE), shaped(half), shaped(half)),
        in_specs=[pl.BlockSpec(memory_space=pltpu.SMEM), VMEM] + [ANY] * 14,
        out_specs=(ANY,) * 4,
        scratch_shapes=[
            pltpu.VMEM(staged, LOW),
            plain,
            turned,
            plain,
            turned,
            square,
            square,
            square,
            turned,
            plain,
            long,
            long,
            long_t,
            long_t,
            pltpu.VMEM(staged, LOW),
            pltpu.VMEM((block, width), WIDE),
            turned,
            turned,
            long,
            long,
            pltpu.VMEM(half, LOW),
            pltpu.VMEM(half, LOW),
            pltpu.SemaphoreType.DMA((16,)),
            pltpu.SemaphoreType.DMA((6,)),
        ],
        compiler_params=pltpu.CompilerParams(vmem_limit_bytes=FULL_VMEM),
        cost_estimate=pl.CostEstimate(
            flops=12 * block * members * width + 32 * members * width * width,
            bytes_accessed=16 * members * width,
            transcendentals=heads * block * members,
        ),
    )(me.reshape(1), log_sum_exp, arrived, *projections, grad_out)
    if not whole_tiles:
        terms = terms.reshape(3, devices, piece, width).transpose(1, 0, 2, 3)
    return terms, own, keep, send


def bits_of(count):
    return [1 << position for position in range(count.bit_length() - 1)]


def stages_of(n_outer, n_inner):
    outer = [mask * n_inner for mask in bits_of(n_outer)]
    inner = bits_of(n_inner)[1:]
    order = []
    for position in range(max(len(outer), len(inner))):
        order += inner[position : position + 1] + outer[position : position + 1]
    return [order[start : start + 2] for start in range(0, len(order), 2)]


def add_up(first, *others):
    total = first.astype(WIDE)
    for other in others:
        total = total + other.astype(WIDE)
    return total


def swap(value, mask, devices):
    return lax.ppermute(value, AXES, [(device, device ^ mask) for device in range(devices)])


def stage_sum(parts, masks, devices):
    got = []
    for index in range(1, len(parts)):
        mask = 0
        for position, each in enumerate(masks):
            if index >> (len(masks) - 1 - position) & 1:
                mask |= each
        got.append(swap(parts[index], mask, devices))
    return parts[0], got


def collect_kernel(partners_ref, returned_ref, summed_ref):
    for node in range(summed_ref.shape[0]):
        total = None
        for match in range(3):
            term = returned_ref[partners_ref[node, match], match].astype(WIDE)
            total = term if total is None else total + term
        summed_ref[node] = total.astype(LOW)


def collect_pieces(returned, partners):
    devices, _, piece, width = returned.shape
    if piece % 8:
        return sum(returned[partners[:, match], match].astype(WIDE) for match in range(3)).astype(LOW)
    return pl.pallas_call(
        collect_kernel,
        out_shape=shaped((devices, piece, width)),
        in_specs=[pl.BlockSpec(memory_space=pltpu.SMEM), VMEM],
        out_specs=VMEM,
        compiler_params=pltpu.CompilerParams(vmem_limit_bytes=FULL_VMEM),
    )(partners, returned)


def on_device(node_feats, grad_out, log_sum_exp, w_query, w_key, w_value, w_output, partners):
    block, width = node_feats.shape
    n_outer, n_inner = lax.axis_size("gx"), lax.axis_size("gy")
    devices = n_outer * n_inner
    piece = block // devices
    me = lax.axis_index("gx") * n_inner + lax.axis_index("gy")
    stages = stages_of(n_outer, n_inner)

    spread = exchange(node_feats.reshape(devices, piece, width))
    arrived = exchange(spread[partners])
    projections = project(node_feats, grad_out, w_query, w_key, w_value, w_output)
    terms, own, keep, send = attention(me, stages, arrived, projections, grad_out, log_sum_exp)
    returned = exchange(terms)
    got = [swap(send, 1, devices)]
    summed = None
    for number, masks in enumerate(stages):
        count = 2 ** len(masks)
        keep = keep.reshape((count, -1) + keep.shape[1:])
        got = [each.reshape(keep.shape) for each in got]
        parts = [
            add_up(keep[index], *(each[index] for each in got)).astype(LOW) for index in range(count)
        ]
        if number == len(stages) - 1:
            summed = collect_pieces(returned, partners)
            *parts, summed = lax.optimization_barrier((*parts, summed))
        keep, got = stage_sum(parts, masks, devices)
    back = exchange(summed).reshape(block, width)
    grad_nodes = (own + back.astype(WIDE)).astype(LOW)
    weight_grads = add_up(keep, *got)[0]
    return grad_nodes, weight_grads


def solution(mesh):
    return jax.shard_map(
        on_device,
        mesh=mesh,
        in_specs=(
            P(AXES, None),
            P(AXES, None),
            P(None, AXES),
            P(),
            P(),
            P(),
            P(),
            P(),
        ),
        out_specs=(P(AXES, None), P("gx", "gy")),
        check_vma=False,
    )
```

```python
import functools
import math

import jax
import jax.numpy as jnp
from jax import lax
from jax.experimental import pallas as pl
from jax.experimental.pallas import tpu as pltpu
from jax.sharding import PartitionSpec as P

AXES = ("gx", "gy")
LOW = jnp.bfloat16
WIDE = jnp.float32


def dot(left, right):
    return jnp.dot(left, right, preferred_element_type=WIDE)


def dot_nt(left, right):
    return lax.dot_general(left, right, (((1,), (1,)), ((), ())), preferred_element_type=WIDE)


def exchange(pieces):
    return lax.all_to_all(pieces, AXES, split_axis=0, concat_axis=0, tiled=True)


VMEM = pl.BlockSpec(memory_space=pltpu.VMEM)
ANY = pl.BlockSpec(memory_space=pl.ANY)
FULL_VMEM = 56 * 1024 * 1024
LITTLE_VMEM = 8 * 1024 * 1024


def shaped(shape, dtype=LOW):
    return jax.ShapeDtypeStruct(shape, dtype)


def project_kernel(
    feats_ref,
    grad_out_ref,
    w_query_ref,
    w_key_ref,
    w_value_ref,
    w_output_ref,
    query_ref,
    query_t_ref,
    d_out_ref,
    d_out_t_ref,
    key_ref,
    key_t_ref,
    value_ref,
    value_t_ref,
    w_query_t_ref,
    w_key_t_ref,
    w_value_t_ref,
    feats_t_ref,
):
    feats = feats_ref[...]
    feats_t_ref[...] = feats.T
    for w_ref, w_t_ref, plain_ref, turned_ref in (
        (w_query_ref, w_query_t_ref, query_ref, query_t_ref),
        (w_key_ref, w_key_t_ref, key_ref, key_t_ref),
        (w_value_ref, w_value_t_ref, value_ref, value_t_ref),
    ):
        w_t = w_ref[...].T
        w_t_ref[...] = w_t
        plain_ref[...] = dot(feats, w_ref[...]).astype(LOW)
        turned_ref[...] = dot_nt(w_t, feats).astype(LOW)
    d_out_ref[...] = dot_nt(grad_out_ref[...], w_output_ref[...]).astype(LOW)
    d_out_t_ref[...] = dot_nt(w_output_ref[...], grad_out_ref[...]).astype(LOW)


def project(node_feats, grad_out, *weights):
    block, width = node_feats.shape
    plain, turned, square = shaped((block, width)), shaped((width, block)), shaped((width, width))
    return pl.pallas_call(
        project_kernel,
        out_shape=(plain, turned) * 4 + (square,) * 3 + (turned,),
        in_specs=[VMEM] * 6,
        out_specs=(VMEM,) * 12,
        compiler_params=pltpu.CompilerParams(vmem_limit_bytes=FULL_VMEM),
        cost_estimate=pl.CostEstimate(
            flops=16 * block * width * width,
            bytes_accessed=2 * (10 * block * width + 7 * width * width),
            transcendentals=0,
        ),
    )(node_feats, grad_out, *weights)


def attention_kernel(
    head_size,
    group,
    chunk,
    stages,
    n_inner,
    me_ref,
    lse_ref,
    arrived_hbm,
    query_hbm,
    query_t_hbm,
    d_out_hbm,
    d_out_t_hbm,
    key_own_hbm,
    key_own_t_hbm,
    value_own_hbm,
    value_own_t_hbm,
    w_query_t_hbm,
    w_key_t_hbm,
    w_value_t_hbm,
    feats_t_hbm,
    grad_out_hbm,
    terms_hbm,
    own_hbm,
    keep_hbm,
    send_hbm,
    arrived_ref,
    query_ref,
    query_t_ref,
    d_out_ref,
    d_out_t_ref,
    w_query_t_ref,
    w_both_t_ref,
    feats_t_ref,
    grad_out_ref,
    key_ref,
    value_ref,
    key_t_ref,
    value_t_ref,
    terms_ref,
    own_ref,
    grad_query_t_ref,
    out_t_ref,
    grad_both_ref,
    keep_ref,
    send_ref,
    prob_ref,
    grad_score_ref,
    in_sem,
    out_sem,
):
    heads = lse_ref.shape[0]
    block, width = query_ref.shape
    members = 4 * block
    scaling = head_size ** (-0.5)
    log2e = math.log2(math.e)

    def by_match(ref, match):
        return ref.at[:, match] if len(ref.shape) == 4 else ref.at[match]

    loads = []

    def load(source, target):
        copy = pltpu.make_async_copy(source, target, in_sem.at[len(loads)])
        copy.start()
        loads.append(copy)
        return copy

    stores = []

    def store(source, target):
        copy = pltpu.make_async_copy(source, target, out_sem.at[len(stores)])
        copy.start()
        stores.append(copy)

    own = pl.ds(0, block)
    first_needs = [
        load(by_match(arrived_hbm, 0), arrived_ref.at[0]),
        load(w_key_t_hbm, w_both_t_ref.at[pl.ds(0, width)]),
    ]
    far_needs = [load(by_match(arrived_hbm, match), arrived_ref.at[match]) for match in (1, 2)]
    value_need = load(w_value_t_hbm, w_both_t_ref.at[pl.ds(width, width)])
    head_needs = [
        load(key_own_hbm, key_ref.at[own]),
        load(query_t_hbm, query_t_ref),
        load(value_own_t_hbm, value_t_ref.at[:, own]),
        load(value_own_hbm, value_ref.at[own]),
        load(d_out_t_hbm, d_out_t_ref),
        load(key_own_t_hbm, key_t_ref.at[:, own]),
        load(query_hbm, query_ref),
        load(d_out_hbm, d_out_ref),
    ]
    last_needs = [
        load(feats_t_hbm, feats_t_ref.at[:, own]),
        load(grad_out_hbm, grad_out_ref),
        load(w_query_t_hbm, w_query_t_ref),
    ]
    for copy in first_needs:
        copy.wait()
    for match in range(3):
        here = slice((match + 1) * block, (match + 2) * block)
        if match > 0:
            far_needs[match - 1].wait()
        far = arrived_ref[match].reshape(block, width)
        key_ref[here] = dot_nt(far, w_both_t_ref[:width]).astype(LOW)
        key_t_ref[:, here] = dot_nt(w_both_t_ref[:width], far).astype(LOW)
        if match == 0:
            value_need.wait()
        value_ref[here] = dot_nt(far, w_both_t_ref[width:]).astype(LOW)
        value_t_ref[:, here] = dot_nt(w_both_t_ref[width:], far).astype(LOW)
        feats_t_ref[:, here] = far.T
    for copy in head_needs:
        copy.wait()
    span = group * head_size
    row = lax.broadcasted_iota(jnp.int32, (span, block), 0) // head_size
    col = lax.broadcasted_iota(jnp.int32, (block, span), 1) // head_size
    for first in range(0, heads, group):
        cols = slice(first * head_size, first * head_size + span)
        query_t = query_t_ref[cols, :]
        d_out_t = d_out_t_ref[cols, :] * scaling
        query = query_ref[:, cols]
        d_out = d_out_ref[:, cols]
        zero_t = jnp.zeros_like(query_t)
        zero = jnp.zeros_like(query)
        for inner in range(group):
            head = first + inner
            rows = slice(head * head_size, (head + 1) * head_size)
            lanes = slice(inner * block, (inner + 1) * block)
            shift = lse_ref[head : head + 1, :] * log2e
            query_one = jnp.where(row == inner, query_t, zero_t)
            for start in range(0, members, chunk):
                here = slice(start, start + chunk)
                score = dot(key_ref[here, cols], query_one)
                prob = jnp.exp2(jnp.minimum(score * (scaling * log2e) - shift, 0.0))
                prob_ref[here, lanes] = prob.astype(LOW)
            out_t = dot(value_t_ref[rows, :], prob_ref[:, lanes]).astype(LOW)
            out_t_ref[rows, :] = out_t
            d_rows = d_out_t_ref[rows, :]
            delta = jnp.sum(d_rows.astype(WIDE) * out_t.astype(WIDE), axis=0, keepdims=True) * scaling
            d_out_one = jnp.where(row == inner, d_out_t, zero_t)
            for start in range(0, members, chunk):
                here = slice(start, start + chunk)
                grad_prob = dot(value_ref[here, cols], d_out_one)
                grad_score = prob_ref[here, lanes].astype(WIDE) * (grad_prob - delta)
                grad_score_ref[here, lanes] = grad_score.astype(LOW)
            grad_query_t_ref[rows, :] = dot(key_t_ref[rows, :], grad_score_ref[:, lanes]).astype(LOW)
        queries = jnp.concatenate([jnp.where(col == inner, query, zero) for inner in range(group)], axis=0)
        d_outs = jnp.concatenate([jnp.where(col == inner, d_out, zero) for inner in range(group)], axis=0)
        for start in range(0, members, chunk):
            here = slice(start, start + chunk)
            grad_both_ref[here, cols] = dot(grad_score_ref[here, :], queries).astype(LOW)
            later = slice(width + cols.start, width + cols.stop)
            grad_both_ref[here, later] = dot(prob_ref[here, :], d_outs).astype(LOW)
    for copy in last_needs:
        copy.wait()

    _, tall, wide = keep_ref.shape
    n_outer = width // tall
    me = me_ref[0]
    odd = me % 2 == 1

    def place(start, total):
        low = total.astype(LOW)
        for offset in range(0, total.shape[1], 2 * wide):
            inner = (start + offset) // wide
            for outer in range(n_outer):
                differ = me ^ (outer * n_inner + inner)
                slot = 0
                for masks in stages:
                    for mask in masks:
                        slot = slot * 2 + jnp.where((differ & mask) != 0, 1, 0)
                here = slice(outer * tall, (outer + 1) * tall)
                left = low[here, offset : offset + wide]
                right = low[here, offset + wide : offset + 2 * wide]
                keep_ref[slot] = jnp.where(odd, right, left)
                send_ref[slot] = jnp.where(odd, left, right)

    place(3 * width, dot(out_t_ref[...], grad_out_ref[...]))
    place(0, dot_nt(feats_t_ref[:, :block], grad_query_t_ref[...]))
    for start in range(0, 2 * width, block):
        place(width + start, dot(feats_t_ref[...], grad_both_ref[:, start : start + block]))
    store(send_ref, send_hbm)
    store(keep_ref, keep_hbm)
    for member in range(4):
        here = slice(member * block, (member + 1) * block)
        total = dot(grad_both_ref[here], w_both_t_ref[...])
        if member == 0:
            own_ref[...] = total + lax.dot_general(
                grad_query_t_ref[...],
                w_query_t_ref[...],
                (((0,), (0,)), ((), ())),
                preferred_element_type=WIDE,
            )
            store(own_ref, own_hbm)
        else:
            terms_ref[member - 1] = total.astype(LOW).reshape(terms_ref.shape[1:])
            store(terms_ref.at[member - 1], by_match(terms_hbm, member - 1))
    for copy in stores:
        copy.wait()


def attention(me, stages, arrived, projections, grad_out, log_sum_exp):
    n_outer, n_inner = lax.axis_size("gx"), lax.axis_size("gy")
    block, width = grad_out.shape
    heads = log_sum_exp.shape[0]
    head_size = width // heads
    members = 4 * block
    group = max(1, 128 // head_size)
    devices, _, piece, _ = arrived.shape
    whole_tiles = piece % 8 == 0
    if not whole_tiles:
        arrived = arrived.transpose(1, 0, 2, 3).reshape(3, block, width)
    staged = (3, devices, piece, width) if whole_tiles else (3, block, width)
    half = (devices // 2, width // n_outer, 4 * width // n_inner)
    plain, turned, square = (
        pltpu.VMEM((block, width), LOW),
        pltpu.VMEM((width, block), LOW),
        pltpu.VMEM((width, width), LOW),
    )
    long, long_t = pltpu.VMEM((members, width), LOW), pltpu.VMEM((width, members), LOW)
    terms, own, keep, send = pl.pallas_call(
        functools.partial(attention_kernel, head_size, group, 2 * block, stages, n_inner),
        out_shape=(shaped(arrived.shape), shaped((block, width), WIDE), shaped(half), shaped(half)),
        in_specs=[pl.BlockSpec(memory_space=pltpu.SMEM), VMEM] + [ANY] * 14,
        out_specs=(ANY,) * 4,
        scratch_shapes=[
            pltpu.VMEM(staged, LOW),
            plain,
            turned,
            plain,
            turned,
            square,
            pltpu.VMEM((2 * width, width), LOW),
            long_t,
            plain,
            long,
            long,
            long_t,
            long_t,
            pltpu.VMEM(staged, LOW),
            pltpu.VMEM((block, width), WIDE),
            turned,
            turned,
            pltpu.VMEM((members, 2 * width), LOW),
            pltpu.VMEM(half, LOW),
            pltpu.VMEM(half, LOW),
            pltpu.VMEM((members, group * block), LOW),
            pltpu.VMEM((members, group * block), LOW),
            pltpu.SemaphoreType.DMA((16,)),
            pltpu.SemaphoreType.DMA((6,)),
        ],
        compiler_params=pltpu.CompilerParams(vmem_limit_bytes=FULL_VMEM),
        cost_estimate=pl.CostEstimate(
            flops=12 * block * members * width + 32 * members * width * width,
            bytes_accessed=16 * members * width,
            transcendentals=heads * block * members,
        ),
    )(me.reshape(1), log_sum_exp, arrived, *projections, grad_out)
    if not whole_tiles:
        terms = terms.reshape(3, devices, piece, width).transpose(1, 0, 2, 3)
    return terms, own, keep, send


def bits_of(count):
    return [1 << position for position in range(count.bit_length() - 1)]


def stages_of(n_outer, n_inner):
    outer = [mask * n_inner for mask in bits_of(n_outer)]
    inner = bits_of(n_inner)[1:]
    order = []
    for position in range(max(len(outer), len(inner))):
        order += inner[position : position + 1] + outer[position : position + 1]
    return [order[start : start + 2] for start in range(0, len(order), 2)]


def add_up(first, *others):
    total = first.astype(WIDE)
    for other in others:
        total = total + other.astype(WIDE)
    return total


def swap(value, mask, devices):
    return lax.ppermute(value, AXES, [(device, device ^ mask) for device in range(devices)])


def stage_sum(parts, masks, devices):
    got = []
    for index in range(1, len(parts)):
        mask = 0
        for position, each in enumerate(masks):
            if index >> (len(masks) - 1 - position) & 1:
                mask |= each
        got.append(swap(parts[index], mask, devices))
    return parts[0], got


def collect_kernel(partners_ref, returned_ref, summed_ref):
    for node in range(summed_ref.shape[0]):
        total = None
        for match in range(3):
            term = returned_ref[partners_ref[node, match], match].astype(WIDE)
            total = term if total is None else total + term
        summed_ref[node] = total.astype(LOW)


def collect_pieces(returned, partners):
    devices, _, piece, width = returned.shape
    if piece % 8:
        return sum(returned[partners[:, match], match].astype(WIDE) for match in range(3)).astype(LOW)
    return pl.pallas_call(
        collect_kernel,
        out_shape=shaped((devices, piece, width)),
        in_specs=[pl.BlockSpec(memory_space=pltpu.SMEM), VMEM],
        out_specs=VMEM,
        compiler_params=pltpu.CompilerParams(vmem_limit_bytes=LITTLE_VMEM),
    )(partners, returned)


def on_device(node_feats, grad_out, log_sum_exp, w_query, w_key, w_value, w_output, partners):
    block, width = node_feats.shape
    n_outer, n_inner = lax.axis_size("gx"), lax.axis_size("gy")
    devices = n_outer * n_inner
    piece = block // devices
    me = lax.axis_index("gx") * n_inner + lax.axis_index("gy")
    stages = stages_of(n_outer, n_inner)

    spread = exchange(node_feats.reshape(devices, piece, width))
    arrived = exchange(spread[partners])
    projections = project(node_feats, grad_out, w_query, w_key, w_value, w_output)
    terms, own, keep, send = attention(me, stages, arrived, projections, grad_out, log_sum_exp)
    returned = exchange(terms)
    got = [swap(send, 1, devices)]
    summed = None
    for number, masks in enumerate(stages):
        count = 2 ** len(masks)
        keep = keep.reshape((count, -1) + keep.shape[1:])
        got = [each.reshape(keep.shape) for each in got]
        parts = [
            add_up(keep[index], *(each[index] for each in got)).astype(LOW) for index in range(count)
        ]
        if number == len(stages) - 1:
            summed = collect_pieces(returned, partners)
        keep, got = stage_sum(parts, masks, devices)
    back = exchange(summed).reshape(block, width)
    grad_nodes = (own + back.astype(WIDE)).astype(LOW)
    weight_grads = add_up(keep, *got)[0]
    return grad_nodes, weight_grads


def solution(mesh):
    return jax.shard_map(
        on_device,
        mesh=mesh,
        in_specs=(
            P(AXES, None),
            P(AXES, None),
            P(None, AXES),
            P(),
            P(),
            P(),
            P(),
            P(),
        ),
        out_specs=(P(AXES, None), P("gx", "gy")),
        check_vma=False,
    )
```

```python
import functools
import math

import jax
import jax.numpy as jnp
from jax import lax
from jax.experimental import pallas as pl
from jax.experimental.pallas import tpu as pltpu
from jax.sharding import PartitionSpec as P

AXES = ("gx", "gy")
LOW = jnp.bfloat16
WIDE = jnp.float32


def dot(left, right):
    return jnp.dot(left, right, preferred_element_type=WIDE)


def dot_nt(left, right):
    return lax.dot_general(left, right, (((1,), (1,)), ((), ())), preferred_element_type=WIDE)


def exchange(pieces):
    return lax.all_to_all(pieces, AXES, split_axis=0, concat_axis=0, tiled=True)


VMEM = pl.BlockSpec(memory_space=pltpu.VMEM)
ANY = pl.BlockSpec(memory_space=pl.ANY)
FULL_VMEM = 56 * 1024 * 1024
LITTLE_VMEM = 8 * 1024 * 1024


def shaped(shape, dtype=LOW):
    return jax.ShapeDtypeStruct(shape, dtype)


def project_kernel(
    feats_ref,
    grad_out_ref,
    w_query_ref,
    w_key_ref,
    w_value_ref,
    w_output_ref,
    query_ref,
    query_t_ref,
    d_out_ref,
    d_out_t_ref,
    key_ref,
    key_t_ref,
    value_ref,
    value_t_ref,
    w_query_t_ref,
    w_key_t_ref,
    w_value_t_ref,
    feats_t_ref,
):
    feats = feats_ref[...]
    feats_t_ref[...] = feats.T
    for w_ref, w_t_ref, plain_ref, turned_ref in (
        (w_query_ref, w_query_t_ref, query_ref, query_t_ref),
        (w_key_ref, w_key_t_ref, key_ref, key_t_ref),
        (w_value_ref, w_value_t_ref, value_ref, value_t_ref),
    ):
        w_t = w_ref[...].T
        w_t_ref[...] = w_t
        plain_ref[...] = dot(feats, w_ref[...]).astype(LOW)
        turned_ref[...] = dot_nt(w_t, feats).astype(LOW)
    d_out_ref[...] = dot_nt(grad_out_ref[...], w_output_ref[...]).astype(LOW)
    d_out_t_ref[...] = dot_nt(w_output_ref[...], grad_out_ref[...]).astype(LOW)


def project(node_feats, grad_out, *weights):
    block, width = node_feats.shape
    plain, turned, square = shaped((block, width)), shaped((width, block)), shaped((width, width))
    return pl.pallas_call(
        project_kernel,
        out_shape=(plain, turned) * 4 + (square,) * 3 + (turned,),
        in_specs=[VMEM] * 6,
        out_specs=(VMEM,) * 12,
        compiler_params=pltpu.CompilerParams(vmem_limit_bytes=FULL_VMEM),
        cost_estimate=pl.CostEstimate(
            flops=16 * block * width * width,
            bytes_accessed=2 * (10 * block * width + 7 * width * width),
            transcendentals=0,
        ),
    )(node_feats, grad_out, *weights)


def attention_kernel(
    head_size,
    group,
    together,
    chunk,
    stages,
    n_inner,
    me_ref,
    lse_ref,
    arrived_hbm,
    query_hbm,
    query_t_hbm,
    d_out_hbm,
    d_out_t_hbm,
    key_own_hbm,
    key_own_t_hbm,
    value_own_hbm,
    value_own_t_hbm,
    w_query_t_hbm,
    w_key_t_hbm,
    w_value_t_hbm,
    feats_t_hbm,
    grad_out_hbm,
    terms_hbm,
    own_hbm,
    keep_hbm,
    send_hbm,
    arrived_ref,
    query_ref,
    query_t_ref,
    d_out_ref,
    d_out_t_ref,
    w_query_t_ref,
    w_both_t_ref,
    feats_t_ref,
    grad_out_ref,
    key_ref,
    value_ref,
    key_t_ref,
    value_t_ref,
    terms_ref,
    own_ref,
    grad_query_t_ref,
    out_t_ref,
    grad_both_ref,
    keep_ref,
    send_ref,
    prob_ref,
    grad_score_ref,
    in_sem,
    out_sem,
):
    heads = lse_ref.shape[0]
    block, width = query_ref.shape
    members = 4 * block
    scaling = head_size ** (-0.5)
    log2e = math.log2(math.e)

    def by_match(ref, match):
        return ref.at[:, match] if len(ref.shape) == 4 else ref.at[match]

    loads = []

    def load(source, target):
        copy = pltpu.make_async_copy(source, target, in_sem.at[len(loads)])
        copy.start()
        loads.append(copy)
        return copy

    stores = []

    def store(source, target):
        copy = pltpu.make_async_copy(source, target, out_sem.at[len(stores)])
        copy.start()
        stores.append(copy)

    own = pl.ds(0, block)
    first_needs = [
        load(by_match(arrived_hbm, 0), arrived_ref.at[0]),
        load(w_key_t_hbm, w_both_t_ref.at[pl.ds(0, width)]),
    ]
    far_needs = [load(by_match(arrived_hbm, match), arrived_ref.at[match]) for match in (1, 2)]
    value_need = load(w_value_t_hbm, w_both_t_ref.at[pl.ds(width, width)])
    head_needs = [
        load(key_own_hbm, key_ref.at[own]),
        load(query_t_hbm, query_t_ref),
        load(value_own_t_hbm, value_t_ref.at[:, own]),
        load(value_own_hbm, value_ref.at[own]),
        load(d_out_t_hbm, d_out_t_ref),
        load(key_own_t_hbm, key_t_ref.at[:, own]),
        load(query_hbm, query_ref),
        load(d_out_hbm, d_out_ref),
    ]
    last_needs = [
        load(feats_t_hbm, feats_t_ref.at[:, own]),
        load(grad_out_hbm, grad_out_ref),
        load(w_query_t_hbm, w_query_t_ref),
    ]
    for copy in first_needs:
        copy.wait()
    for match in range(3):
        here = slice((match + 1) * block, (match + 2) * block)
        if match > 0:
            far_needs[match - 1].wait()
        far = arrived_ref[match].reshape(block, width)
        far_key = dot_nt(far, w_both_t_ref[:width]).astype(LOW)
        key_ref[here] = far_key
        key_t_ref[:, here] = far_key.T
        if match == 0:
            value_need.wait()
        far_value = dot_nt(far, w_both_t_ref[width:]).astype(LOW)
        value_ref[here] = far_value
        value_t_ref[:, here] = far_value.T
        feats_t_ref[:, here] = far.T
    for copy in head_needs:
        copy.wait()
    span = group * head_size
    row = lax.broadcasted_iota(jnp.int32, (span, block), 0) // head_size
    col = lax.broadcasted_iota(jnp.int32, (block, span), 1) // head_size
    for batch in range(0, heads, together):
        batch_heads = range(batch, batch + together)
        deltas = {}

        def places(head):
            first = head - head % group
            cols = slice(first * head_size, first * head_size + span)
            rows = slice(head * head_size, (head + 1) * head_size)
            lanes = slice((head - batch) * block, (head - batch + 1) * block)
            return head % group, cols, rows, lanes

        for head in batch_heads:
            inner, cols, rows, lanes = places(head)
            shift = lse_ref[head : head + 1, :] * log2e
            query_t = query_t_ref[cols, :]
            query_one = jnp.where(row == inner, query_t, jnp.zeros_like(query_t))
            for start in range(0, members, chunk):
                here = slice(start, start + chunk)
                score = dot(key_ref[here, cols], query_one)
                prob = jnp.exp2(jnp.minimum(score * (scaling * log2e) - shift, 0.0))
                prob_ref[here, lanes] = prob.astype(LOW)
        for head in batch_heads:
            inner, cols, rows, lanes = places(head)
            out_t = dot(value_t_ref[rows, :], prob_ref[:, lanes]).astype(LOW)
            out_t_ref[rows, :] = out_t
            d_rows = d_out_t_ref[rows, :].astype(WIDE)
            deltas[head] = jnp.sum(d_rows * out_t.astype(WIDE), axis=0, keepdims=True) * scaling
        for head in batch_heads:
            inner, cols, rows, lanes = places(head)
            d_out_t = d_out_t_ref[cols, :] * scaling
            d_out_one = jnp.where(row == inner, d_out_t, jnp.zeros_like(d_out_t))
            for start in range(0, members, chunk):
                here = slice(start, start + chunk)
                grad_prob = dot(value_ref[here, cols], d_out_one)
                grad_score = prob_ref[here, lanes].astype(WIDE) * (grad_prob - deltas[head])
                grad_score_ref[here, lanes] = grad_score.astype(LOW)
        for first in range(batch, batch + together, group):
            _, cols, _, _ = places(first)
            later = slice(width + cols.start, width + cols.stop)
            lanes = slice((first - batch) * block, (first - batch + group) * block)
            query, d_out = query_ref[:, cols], d_out_ref[:, cols]
            queries = [jnp.where(col == inner, query, jnp.zeros_like(query)) for inner in range(group)]
            d_outs = [jnp.where(col == inner, d_out, jnp.zeros_like(d_out)) for inner in range(group)]
            queries, d_outs = jnp.concatenate(queries, axis=0), jnp.concatenate(d_outs, axis=0)
            for start in range(0, members, chunk):
                here = slice(start, start + chunk)
                grad_both_ref[here, cols] = dot(grad_score_ref[here, lanes], queries).astype(LOW)
                grad_both_ref[here, later] = dot(prob_ref[here, lanes], d_outs).astype(LOW)
        for head in batch_heads:
            inner, cols, rows, lanes = places(head)
            grad_query_t_ref[rows, :] = dot(key_t_ref[rows, :], grad_score_ref[:, lanes]).astype(LOW)
    for copy in last_needs:
        copy.wait()

    _, tall, wide = keep_ref.shape
    n_outer = width // tall
    me = me_ref[0]
    odd = me % 2 == 1

    def place(start, total):
        low = total.astype(LOW)
        for offset in range(0, total.shape[1], 2 * wide):
            inner = (start + offset) // wide
            for outer in range(n_outer):
                differ = me ^ (outer * n_inner + inner)
                slot = 0
                for masks in stages:
                    for mask in masks:
                        slot = slot * 2 + jnp.where((differ & mask) != 0, 1, 0)
                here = slice(outer * tall, (outer + 1) * tall)
                left = low[here, offset : offset + wide]
                right = low[here, offset + wide : offset + 2 * wide]
                keep_ref[slot] = jnp.where(odd, right, left)
                send_ref[slot] = jnp.where(odd, left, right)

    place(3 * width, dot(out_t_ref[...], grad_out_ref[...]))
    place(0, dot_nt(feats_t_ref[:, :block], grad_query_t_ref[...]))
    for start in range(0, 2 * width, block):
        place(width + start, dot(feats_t_ref[...], grad_both_ref[:, start : start + block]))
    store(send_ref, send_hbm)
    store(keep_ref, keep_hbm)
    for member in range(4):
        here = slice(member * block, (member + 1) * block)
        total = dot(grad_both_ref[here], w_both_t_ref[...])
        if member == 0:
            own_ref[...] = total + lax.dot_general(
                grad_query_t_ref[...],
                w_query_t_ref[...],
                (((0,), (0,)), ((), ())),
                preferred_element_type=WIDE,
            )
            store(own_ref, own_hbm)
        else:
            terms_ref[member - 1] = total.astype(LOW).reshape(terms_ref.shape[1:])
            store(terms_ref.at[member - 1], by_match(terms_hbm, member - 1))
    for copy in stores:
        copy.wait()


def attention(me, stages, arrived, projections, grad_out, log_sum_exp):
    n_outer, n_inner = lax.axis_size("gx"), lax.axis_size("gy")
    block, width = grad_out.shape
    heads = log_sum_exp.shape[0]
    head_size = width // heads
    members = 4 * block
    group = max(1, 128 // head_size)
    together = min(heads, group)
    devices, _, piece, _ = arrived.shape
    whole_tiles = piece % 8 == 0
    if not whole_tiles:
        arrived = arrived.transpose(1, 0, 2, 3).reshape(3, block, width)
    staged = (3, devices, piece, width) if whole_tiles else (3, block, width)
    half = (devices // 2, width // n_outer, 4 * width // n_inner)
    plain, turned, square = (
        pltpu.VMEM((block, width), LOW),
        pltpu.VMEM((width, block), LOW),
        pltpu.VMEM((width, width), LOW),
    )
    long, long_t = pltpu.VMEM((members, width), LOW), pltpu.VMEM((width, members), LOW)
    terms, own, keep, send = pl.pallas_call(
        functools.partial(attention_kernel, head_size, group, together, 2 * block, stages, n_inner),
        out_shape=(shaped(arrived.shape), shaped((block, width), WIDE), shaped(half), shaped(half)),
        in_specs=[pl.BlockSpec(memory_space=pltpu.SMEM), VMEM] + [ANY] * 14,
        out_specs=(ANY,) * 4,
        scratch_shapes=[
            pltpu.VMEM(staged, LOW),
            plain,
            turned,
            plain,
            turned,
            square,
            pltpu.VMEM((2 * width, width), LOW),
            long_t,
            plain,
            long,
            long,
            long_t,
            long_t,
            pltpu.VMEM(staged, LOW),
            pltpu.VMEM((block, width), WIDE),
            turned,
            turned,
            pltpu.VMEM((members, 2 * width), LOW),
            pltpu.VMEM(half, LOW),
            pltpu.VMEM(half, LOW),
            pltpu.VMEM((members, together * block), LOW),
            pltpu.VMEM((members, together * block), LOW),
            pltpu.SemaphoreType.DMA((16,)),
            pltpu.SemaphoreType.DMA((6,)),
        ],
        compiler_params=pltpu.CompilerParams(vmem_limit_bytes=FULL_VMEM),
        cost_estimate=pl.CostEstimate(
            flops=12 * block * members * width + 32 * members * width * width,
            bytes_accessed=16 * members * width,
            transcendentals=heads * block * members,
        ),
    )(me.reshape(1), log_sum_exp, arrived, *projections, grad_out)
    if not whole_tiles:
        terms = terms.reshape(3, devices, piece, width).transpose(1, 0, 2, 3)
    return terms, own, keep, send


def bits_of(count):
    return [1 << position for position in range(count.bit_length() - 1)]


def stages_of(n_outer, n_inner):
    outer = [mask * n_inner for mask in bits_of(n_outer)]
    inner = bits_of(n_inner)[1:]
    order = []
    for position in range(max(len(outer), len(inner))):
        order += inner[position : position + 1] + outer[position : position + 1]
    return [order[start : start + 2] for start in range(0, len(order), 2)]


def add_up(first, *others):
    total = first.astype(WIDE)
    for other in others:
        total = total + other.astype(WIDE)
    return total


def swap(value, mask, devices):
    return lax.ppermute(value, AXES, [(device, device ^ mask) for device in range(devices)])


def stage_sum(parts, masks, devices):
    got = []
    for index in range(1, len(parts)):
        mask = 0
        for position, each in enumerate(masks):
            if index >> (len(masks) - 1 - position) & 1:
                mask |= each
        got.append(swap(parts[index], mask, devices))
    return parts[0], got


def collect_kernel(partners_ref, returned_ref, summed_ref):
    for node in range(summed_ref.shape[0]):
        total = None
        for match in range(3):
            term = returned_ref[partners_ref[node, match], match].astype(WIDE)
            total = term if total is None else total + term
        summed_ref[node] = total.astype(LOW)


def collect_pieces(returned, partners):
    devices, _, piece, width = returned.shape
    if piece % 8:
        return sum(returned[partners[:, match], match].astype(WIDE) for match in range(3)).astype(LOW)
    return pl.pallas_call(
        collect_kernel,
        out_shape=shaped((devices, piece, width)),
        in_specs=[pl.BlockSpec(memory_space=pltpu.SMEM), VMEM],
        out_specs=VMEM,
        compiler_params=pltpu.CompilerParams(vmem_limit_bytes=LITTLE_VMEM),
    )(partners, returned)


def on_device(node_feats, grad_out, log_sum_exp, w_query, w_key, w_value, w_output, partners):
    block, width = node_feats.shape
    n_outer, n_inner = lax.axis_size("gx"), lax.axis_size("gy")
    devices = n_outer * n_inner
    piece = block // devices
    me = lax.axis_index("gx") * n_inner + lax.axis_index("gy")
    stages = stages_of(n_outer, n_inner)

    spread = exchange(node_feats.reshape(devices, piece, width))
    arrived = exchange(spread[partners])
    projections = project(node_feats, grad_out, w_query, w_key, w_value, w_output)
    terms, own, keep, send = attention(me, stages, arrived, projections, grad_out, log_sum_exp)
    returned = exchange(terms)
    got = [swap(send, 1, devices)]
    summed = None
    for number, masks in enumerate(stages):
        count = 2 ** len(masks)
        keep = keep.reshape((count, -1) + keep.shape[1:])
        got = [each.reshape(keep.shape) for each in got]
        parts = [
            add_up(keep[index], *(each[index] for each in got)).astype(LOW) for index in range(count)
        ]
        if number == len(stages) - 1:
            summed = collect_pieces(returned, partners)
        keep, got = stage_sum(parts, masks, devices)
    back = exchange(summed).reshape(block, width)
    grad_nodes = (own + back.astype(WIDE)).astype(LOW)
    weight_grads = add_up(keep, *got)[0]
    return grad_nodes, weight_grads


def solution(mesh):
    return jax.shard_map(
        on_device,
        mesh=mesh,
        in_specs=(
            P(AXES, None),
            P(AXES, None),
            P(None, AXES),
            P(),
            P(),
            P(),
            P(),
            P(),
        ),
        out_specs=(P(AXES, None), P("gx", "gy")),
        check_vma=False,
    )
```

```python
import functools
import math

import jax
import jax.numpy as jnp
from jax import lax
from jax.experimental import pallas as pl
from jax.experimental.pallas import tpu as pltpu
from jax.sharding import PartitionSpec as P

AXES = ("gx", "gy")
LOW = jnp.bfloat16
WIDE = jnp.float32


def dot(left, right):
    return jnp.dot(left, right, preferred_element_type=WIDE)


def dot_nt(left, right):
    return lax.dot_general(left, right, (((1,), (1,)), ((), ())), preferred_element_type=WIDE)


def exchange(pieces):
    return lax.all_to_all(pieces, AXES, split_axis=0, concat_axis=0, tiled=True)


VMEM = pl.BlockSpec(memory_space=pltpu.VMEM)
ANY = pl.BlockSpec(memory_space=pl.ANY)
FULL_VMEM = 56 * 1024 * 1024
MOST_VMEM = 50 * 1024 * 1024
LITTLE_VMEM = 8 * 1024 * 1024


def shaped(shape, dtype=LOW):
    return jax.ShapeDtypeStruct(shape, dtype)


def packing(block, width):
    rows, places = 0, {}
    for name in ("w_key_t", "w_value_t", "w_query_t"):
        places[name] = (pl.ds(rows, width), pl.ds(0, width))
        rows += width
    for name in ("query", "d_out", "key", "value", "grad_out"):
        places[name] = (pl.ds(rows, block), pl.ds(0, width))
        rows += block
    for pair in (("query_t", "d_out_t"), ("key_t", "value_t"), ("feats_t",)):
        for position, name in enumerate(pair):
            places[name] = (pl.ds(rows, width), pl.ds(position * block, block))
        rows += width
    return rows, places


def project_kernel(
    feats_ref, grad_out_ref, w_query_ref, w_key_ref, w_value_ref, w_output_ref, packed_ref
):
    block, width = feats_ref.shape
    _, places = packing(block, width)

    def put(name, value):
        packed_ref[places[name]] = value.astype(LOW)

    feats = feats_ref[...]
    grad_out = grad_out_ref[...]
    put("feats_t", feats.T)
    put("grad_out", grad_out)
    for name, w_ref in (("query", w_query_ref), ("key", w_key_ref), ("value", w_value_ref)):
        put("w_" + name + "_t", w_ref[...].T)
        projected = dot(feats, w_ref[...]).astype(LOW)
        put(name, projected)
        put(name + "_t", projected.T)
    d_out = dot_nt(grad_out, w_output_ref[...]).astype(LOW)
    put("d_out", d_out)
    put("d_out_t", d_out.T)


def project(node_feats, grad_out, *weights):
    block, width = node_feats.shape
    rows, _ = packing(block, width)
    return pl.pallas_call(
        project_kernel,
        out_shape=shaped((rows, width)),
        in_specs=[VMEM] * 6,
        out_specs=VMEM,
        compiler_params=pltpu.CompilerParams(vmem_limit_bytes=FULL_VMEM),
        cost_estimate=pl.CostEstimate(
            flops=8 * block * width * width,
            bytes_accessed=2 * (10 * block * width + 7 * width * width),
            transcendentals=0,
        ),
    )(node_feats, grad_out, *weights)


def attention_kernel(
    head_size,
    group,
    together,
    chunk,
    stages,
    n_inner,
    me_ref,
    lse_hbm,
    arrived_ref,
    packed_hbm,
    terms_hbm,
    own_hbm,
    keep_hbm,
    send_hbm,
    query_ref,
    query_t_ref,
    d_out_ref,
    d_out_t_ref,
    w_query_t_ref,
    w_both_t_ref,
    feats_t_ref,
    grad_out_ref,
    key_ref,
    value_ref,
    key_t_ref,
    value_t_ref,
    terms_ref,
    own_ref,
    grad_query_t_ref,
    out_t_ref,
    grad_both_ref,
    keep_ref,
    send_ref,
    prob_ref,
    grad_score_ref,
    lse_ref,
    in_sem,
    out_sem,
):
    heads = lse_ref.shape[0]
    block, width = query_ref.shape
    members = 4 * block
    scaling = head_size ** (-0.5)
    log2e = math.log2(math.e)

    def by_match(ref, match):
        return ref.at[:, match] if len(ref.shape) == 4 else ref.at[match]

    loads = []

    def load(source, target):
        copy = pltpu.make_async_copy(source, target, in_sem.at[len(loads)])
        copy.start()
        loads.append(copy)
        return copy

    stores = []

    def store(source, target):
        copy = pltpu.make_async_copy(source, target, out_sem.at[len(stores)])
        copy.start()
        stores.append(copy)

    _, places = packing(block, width)

    def part(name):
        return packed_hbm.at[places[name]]

    def far_rows(match):
        rows = arrived_ref[:, match] if len(arrived_ref.shape) == 4 else arrived_ref[match]
        return rows.reshape(block, width)

    own = pl.ds(0, block)
    key_need = load(part("w_key_t"), w_both_t_ref.at[pl.ds(0, width)])
    value_need = load(part("w_value_t"), w_both_t_ref.at[pl.ds(width, width)])
    head_needs = [
        load(lse_hbm, lse_ref),
        load(part("key"), key_ref.at[own]),
        load(part("query_t"), query_t_ref),
        load(part("value_t"), value_t_ref.at[:, own]),
        load(part("value"), value_ref.at[own]),
        load(part("d_out_t"), d_out_t_ref),
        load(part("key_t"), key_t_ref.at[:, own]),
        load(part("query"), query_ref),
        load(part("d_out"), d_out_ref),
    ]
    last_needs = [
        load(part("feats_t"), feats_t_ref.at[:, own]),
        load(part("grad_out"), grad_out_ref),
        load(part("w_query_t"), w_query_t_ref),
    ]
    key_need.wait()
    for match in range(3):
        here = slice((match + 1) * block, (match + 2) * block)
        far = far_rows(match)
        far_key = dot_nt(far, w_both_t_ref[:width]).astype(LOW)
        key_ref[here] = far_key
        key_t_ref[:, here] = far_key.T
        if match == 0:
            value_need.wait()
        far_value = dot_nt(far, w_both_t_ref[width:]).astype(LOW)
        value_ref[here] = far_value
        value_t_ref[:, here] = far_value.T
        feats_t_ref[:, here] = far.T
    for copy in head_needs:
        copy.wait()
    span = group * head_size
    row = lax.broadcasted_iota(jnp.int32, (span, block), 0) // head_size
    col = lax.broadcasted_iota(jnp.int32, (block, span), 1) // head_size
    for batch in range(0, heads, together):
        batch_heads = range(batch, batch + together)
        deltas = {}

        def places(head):
            first = head - head % group
            cols = slice(first * head_size, first * head_size + span)
            rows = slice(head * head_size, (head + 1) * head_size)
            lanes = slice((head - batch) * block, (head - batch + 1) * block)
            return head % group, cols, rows, lanes

        for head in batch_heads:
            inner, cols, rows, lanes = places(head)
            shift = lse_ref[head : head + 1, :] * log2e
            query_t = query_t_ref[cols, :]
            query_one = jnp.where(row == inner, query_t, jnp.zeros_like(query_t))
            for start in range(0, members, chunk):
                here = slice(start, start + chunk)
                score = dot(key_ref[here, cols], query_one)
                prob = jnp.exp2(jnp.minimum(score * (scaling * log2e) - shift, 0.0))
                prob_ref[here, lanes] = prob.astype(LOW)
        for head in batch_heads:
            inner, cols, rows, lanes = places(head)
            out_t = dot(value_t_ref[rows, :], prob_ref[:, lanes]).astype(LOW)
            out_t_ref[rows, :] = out_t
            d_rows = d_out_t_ref[rows, :].astype(WIDE)
            deltas[head] = jnp.sum(d_rows * out_t.astype(WIDE), axis=0, keepdims=True) * scaling
        for head in batch_heads:
            inner, cols, rows, lanes = places(head)
            d_out_t = d_out_t_ref[cols, :] * scaling
            d_out_one = jnp.where(row == inner, d_out_t, jnp.zeros_like(d_out_t))
            for start in range(0, members, chunk):
                here = slice(start, start + chunk)
                grad_prob = dot(value_ref[here, cols], d_out_one)
                grad_score = prob_ref[here, lanes].astype(WIDE) * (grad_prob - deltas[head])
                grad_score_ref[here, lanes] = grad_score.astype(LOW)
        for first in range(batch, batch + together, group):
            _, cols, _, _ = places(first)
            later = slice(width + cols.start, width + cols.stop)
            lanes = slice((first - batch) * block, (first - batch + group) * block)
            query, d_out = query_ref[:, cols], d_out_ref[:, cols]
            queries = [jnp.where(col == inner, query, jnp.zeros_like(query)) for inner in range(group)]
            d_outs = [jnp.where(col == inner, d_out, jnp.zeros_like(d_out)) for inner in range(group)]
            queries, d_outs = jnp.concatenate(queries, axis=0), jnp.concatenate(d_outs, axis=0)
            for start in range(0, members, chunk):
                here = slice(start, start + chunk)
                grad_both_ref[here, cols] = dot(grad_score_ref[here, lanes], queries).astype(LOW)
                grad_both_ref[here, later] = dot(prob_ref[here, lanes], d_outs).astype(LOW)
        for head in batch_heads:
            inner, cols, rows, lanes = places(head)
            grad_query_t_ref[rows, :] = dot(key_t_ref[rows, :], grad_score_ref[:, lanes]).astype(LOW)
    for copy in last_needs:
        copy.wait()

    _, tall, wide = keep_ref.shape
    n_outer = width // tall
    me = me_ref[0]
    odd = me % 2 == 1

    def place(start, total):
        low = total.astype(LOW)
        for offset in range(0, total.shape[1], 2 * wide):
            inner = (start + offset) // wide
            for outer in range(n_outer):
                differ = me ^ (outer * n_inner + inner)
                slot = 0
                for masks in stages:
                    for mask in masks:
                        slot = slot * 2 + jnp.where((differ & mask) != 0, 1, 0)
                here = slice(outer * tall, (outer + 1) * tall)
                left = low[here, offset : offset + wide]
                right = low[here, offset + wide : offset + 2 * wide]
                keep_ref[slot] = jnp.where(odd, right, left)
                send_ref[slot] = jnp.where(odd, left, right)

    place(3 * width, dot(out_t_ref[...], grad_out_ref[...]))
    place(0, dot_nt(feats_t_ref[:, :block], grad_query_t_ref[...]))
    for start in range(0, 2 * width, block):
        place(width + start, dot(feats_t_ref[...], grad_both_ref[:, start : start + block]))
    store(send_ref, send_hbm)
    store(keep_ref, keep_hbm)
    for member in range(4):
        here = slice(member * block, (member + 1) * block)
        total = dot(grad_both_ref[here], w_both_t_ref[...])
        if member == 0:
            own_ref[...] = total + lax.dot_general(
                grad_query_t_ref[...],
                w_query_t_ref[...],
                (((0,), (0,)), ((), ())),
                preferred_element_type=WIDE,
            )
            store(own_ref, own_hbm)
        else:
            terms_ref[member - 1] = total.astype(LOW).reshape(terms_ref.shape[1:])
            store(terms_ref.at[member - 1], by_match(terms_hbm, member - 1))
    for copy in stores:
        copy.wait()


def attention(me, stages, arrived, packed, block, width, log_sum_exp):
    n_outer, n_inner = lax.axis_size("gx"), lax.axis_size("gy")
    heads = log_sum_exp.shape[0]
    head_size = width // heads
    members = 4 * block
    group = max(1, 128 // head_size)
    together = min(heads, group)
    devices, _, piece, _ = arrived.shape
    whole_tiles = piece % 8 == 0
    if not whole_tiles:
        arrived = arrived.transpose(1, 0, 2, 3).reshape(3, block, width)
    staged = (3, devices, piece, width) if whole_tiles else (3, block, width)
    half = (devices // 2, width // n_outer, 4 * width // n_inner)
    plain, turned, square = (
        pltpu.VMEM((block, width), LOW),
        pltpu.VMEM((width, block), LOW),
        pltpu.VMEM((width, width), LOW),
    )
    long, long_t = pltpu.VMEM((members, width), LOW), pltpu.VMEM((width, members), LOW)
    terms, own, keep, send = pl.pallas_call(
        functools.partial(attention_kernel, head_size, group, together, 2 * block, stages, n_inner),
        out_shape=(shaped(arrived.shape), shaped((block, width), WIDE), shaped(half), shaped(half)),
        in_specs=[pl.BlockSpec(memory_space=pltpu.SMEM), ANY, VMEM, ANY],
        out_specs=(ANY,) * 4,
        scratch_shapes=[
            plain,
            turned,
            plain,
            turned,
            square,
            pltpu.VMEM((2 * width, width), LOW),
            long_t,
            plain,
            long,
            long,
            long_t,
            long_t,
            pltpu.VMEM(staged, LOW),
            pltpu.VMEM((block, width), WIDE),
            turned,
            turned,
            pltpu.VMEM((members, 2 * width), LOW),
            pltpu.VMEM(half, LOW),
            pltpu.VMEM(half, LOW),
            pltpu.VMEM((members, together * block), LOW),
            pltpu.VMEM((members, together * block), LOW),
            pltpu.VMEM((heads, block), WIDE),
            pltpu.SemaphoreType.DMA((17,)),
            pltpu.SemaphoreType.DMA((6,)),
        ],
        compiler_params=pltpu.CompilerParams(vmem_limit_bytes=MOST_VMEM),
        cost_estimate=pl.CostEstimate(
            flops=12 * block * members * width + 32 * members * width * width,
            bytes_accessed=16 * members * width,
            transcendentals=heads * block * members,
        ),
    )(me.reshape(1), log_sum_exp, arrived, packed)
    if not whole_tiles:
        terms = terms.reshape(3, devices, piece, width).transpose(1, 0, 2, 3)
    return terms, own, keep, send


def bits_of(count):
    return [1 << position for position in range(count.bit_length() - 1)]


def stages_of(n_outer, n_inner):
    outer = [mask * n_inner for mask in bits_of(n_outer)]
    inner = bits_of(n_inner)[1:]
    order = []
    for position in range(max(len(outer), len(inner))):
        order += inner[position : position + 1] + outer[position : position + 1]
    return [order[start : start + 2] for start in range(0, len(order), 2)]


def add_up(first, *others):
    total = first.astype(WIDE)
    for other in others:
        total = total + other.astype(WIDE)
    return total


def swap(value, mask, devices):
    return lax.ppermute(value, AXES, [(device, device ^ mask) for device in range(devices)])


def stage_sum(parts, masks, devices):
    got = []
    for index in range(1, len(parts)):
        mask = 0
        for position, each in enumerate(masks):
            if index >> (len(masks) - 1 - position) & 1:
                mask |= each
        got.append(swap(parts[index], mask, devices))
    return parts[0], got


def collect_kernel(partners_ref, returned_ref, summed_ref):
    for node in range(summed_ref.shape[0]):
        total = None
        for match in range(3):
            term = returned_ref[partners_ref[node, match], match].astype(WIDE)
            total = term if total is None else total + term
        summed_ref[node] = total.astype(LOW)


def collect_pieces(returned, partners):
    devices, _, piece, width = returned.shape
    if piece % 8:
        return sum(returned[partners[:, match], match].astype(WIDE) for match in range(3)).astype(LOW)
    return pl.pallas_call(
        collect_kernel,
        out_shape=shaped((devices, piece, width)),
        in_specs=[pl.BlockSpec(memory_space=pltpu.SMEM), VMEM],
        out_specs=VMEM,
        compiler_params=pltpu.CompilerParams(vmem_limit_bytes=LITTLE_VMEM),
    )(partners, returned)


def on_device(node_feats, grad_out, log_sum_exp, w_query, w_key, w_value, w_output, partners):
    block, width = node_feats.shape
    n_outer, n_inner = lax.axis_size("gx"), lax.axis_size("gy")
    devices = n_outer * n_inner
    piece = block // devices
    me = lax.axis_index("gx") * n_inner + lax.axis_index("gy")
    stages = stages_of(n_outer, n_inner)

    spread = exchange(node_feats.reshape(devices, piece, width))
    arrived = exchange(spread[partners])
    packed = project(node_feats, grad_out, w_query, w_key, w_value, w_output)
    terms, own, keep, send = attention(me, stages, arrived, packed, block, width, log_sum_exp)
    returned = exchange(terms)
    got = [swap(send, 1, devices)]
    summed = None
    for number, masks in enumerate(stages):
        count = 2 ** len(masks)
        keep = keep.reshape((count, -1) + keep.shape[1:])
        got = [each.reshape(keep.shape) for each in got]
        parts = [
            add_up(keep[index], *(each[index] for each in got)).astype(LOW) for index in range(count)
        ]
        if number == len(stages) - 1:
            summed = collect_pieces(returned, partners)
        keep, got = stage_sum(parts, masks, devices)
    back = exchange(summed).reshape(block, width)
    grad_nodes = (own + back.astype(WIDE)).astype(LOW)
    weight_grads = add_up(keep, *got)[0]
    return grad_nodes, weight_grads


def solution(mesh):
    return jax.shard_map(
        on_device,
        mesh=mesh,
        in_specs=(
            P(AXES, None),
            P(AXES, None),
            P(None, AXES),
            P(),
            P(),
            P(),
            P(),
            P(),
        ),
        out_specs=(P(AXES, None), P("gx", "gy")),
        check_vma=False,
    )
```

```python
import functools
import math

import jax
import jax.numpy as jnp
from jax import lax
from jax.experimental import pallas as pl
from jax.experimental.pallas import tpu as pltpu
from jax.sharding import PartitionSpec as P

AXES = ("gx", "gy")
LOW = jnp.bfloat16
WIDE = jnp.float32


def dot(left, right):
    return jnp.dot(left, right, preferred_element_type=WIDE)


def dot_nt(left, right):
    return lax.dot_general(left, right, (((1,), (1,)), ((), ())), preferred_element_type=WIDE)


def exchange(pieces):
    return lax.all_to_all(pieces, AXES, split_axis=0, concat_axis=0, tiled=True)


VMEM = pl.BlockSpec(memory_space=pltpu.VMEM)
ANY = pl.BlockSpec(memory_space=pl.ANY)
FULL_VMEM = 56 * 1024 * 1024
MOST_VMEM = 50 * 1024 * 1024
LITTLE_VMEM = 8 * 1024 * 1024


def shaped(shape, dtype=LOW):
    return jax.ShapeDtypeStruct(shape, dtype)


def packing(block, width):
    rows, places = 0, {}
    for name in ("w_key_t", "w_value_t", "w_query_t"):
        places[name] = (pl.ds(rows, width), pl.ds(0, width))
        rows += width
    for name in ("query", "d_out", "key", "value", "grad_out"):
        places[name] = (pl.ds(rows, block), pl.ds(0, width))
        rows += block
    for pair in (("query_t", "d_out_t"), ("key_t", "value_t"), ("feats_t",)):
        for position, name in enumerate(pair):
            places[name] = (pl.ds(rows, width), pl.ds(position * block, block))
        rows += width
    return rows, places


def project_kernel(
    feats_ref, grad_out_ref, w_query_ref, w_key_ref, w_value_ref, w_output_ref, packed_ref
):
    block, width = feats_ref.shape
    _, places = packing(block, width)

    def put(name, value):
        packed_ref[places[name]] = value.astype(LOW)

    feats = feats_ref[...]
    grad_out = grad_out_ref[...]
    put("feats_t", feats.T)
    put("grad_out", grad_out)
    for name, w_ref in (("query", w_query_ref), ("key", w_key_ref), ("value", w_value_ref)):
        put("w_" + name + "_t", w_ref[...].T)
        projected = dot(feats, w_ref[...]).astype(LOW)
        put(name, projected)
        put(name + "_t", projected.T)
    d_out = dot_nt(grad_out, w_output_ref[...]).astype(LOW)
    put("d_out", d_out)
    put("d_out_t", d_out.T)


def project(node_feats, grad_out, *weights):
    block, width = node_feats.shape
    rows, _ = packing(block, width)
    return pl.pallas_call(
        project_kernel,
        out_shape=shaped((rows, width)),
        in_specs=[VMEM] * 6,
        out_specs=VMEM,
        compiler_params=pltpu.CompilerParams(vmem_limit_bytes=FULL_VMEM),
        cost_estimate=pl.CostEstimate(
            flops=8 * block * width * width,
            bytes_accessed=2 * (10 * block * width + 7 * width * width),
            transcendentals=0,
        ),
    )(node_feats, grad_out, *weights)


def attention_kernel(
    head_size,
    group,
    together,
    chunk,
    stages,
    n_inner,
    me_ref,
    lse_hbm,
    arrived_ref,
    packed_hbm,
    terms_hbm,
    own_hbm,
    keep_hbm,
    send_hbm,
    query_ref,
    query_t_ref,
    d_out_ref,
    d_out_t_ref,
    w_query_t_ref,
    w_both_t_ref,
    feats_t_ref,
    grad_out_ref,
    key_ref,
    value_ref,
    key_t_ref,
    value_t_ref,
    terms_ref,
    own_ref,
    grad_query_t_ref,
    out_t_ref,
    grad_both_ref,
    keep_ref,
    send_ref,
    prob_ref,
    grad_score_ref,
    lse_ref,
    in_sem,
    out_sem,
):
    heads = lse_ref.shape[0]
    block, width = query_ref.shape
    members = 4 * block
    scaling = head_size ** (-0.5)
    log2e = math.log2(math.e)

    def by_match(ref, match):
        return ref.at[:, match] if len(ref.shape) == 4 else ref.at[match]

    loads = []

    def load(source, target):
        copy = pltpu.make_async_copy(source, target, in_sem.at[len(loads)])
        copy.start()
        loads.append(copy)
        return copy

    stores = []

    def store(source, target):
        copy = pltpu.make_async_copy(source, target, out_sem.at[len(stores)])
        copy.start()
        stores.append(copy)

    _, places = packing(block, width)

    def part(name):
        return packed_hbm.at[places[name]]

    def far_rows(match):
        rows = arrived_ref[:, match] if len(arrived_ref.shape) == 4 else arrived_ref[match]
        return rows.reshape(block, width)

    own = pl.ds(0, block)
    key_need = load(part("w_key_t"), w_both_t_ref.at[pl.ds(0, width)])
    value_need = load(part("w_value_t"), w_both_t_ref.at[pl.ds(width, width)])
    head_needs = [
        load(lse_hbm, lse_ref),
        load(part("key"), key_ref.at[own]),
        load(part("query_t"), query_t_ref),
        load(part("value_t"), value_t_ref.at[:, own]),
        load(part("value"), value_ref.at[own]),
        load(part("d_out_t"), d_out_t_ref),
        load(part("key_t"), key_t_ref.at[:, own]),
        load(part("query"), query_ref),
        load(part("d_out"), d_out_ref),
    ]
    last_needs = [
        load(part("feats_t"), feats_t_ref.at[:, own]),
        load(part("grad_out"), grad_out_ref),
        load(part("w_query_t"), w_query_t_ref),
    ]
    key_need.wait()
    for match in range(3):
        here = slice((match + 1) * block, (match + 2) * block)
        far = far_rows(match)
        far_key = dot_nt(far, w_both_t_ref[:width]).astype(LOW)
        key_ref[here] = far_key
        key_t_ref[:, here] = far_key.T
        if match == 0:
            value_need.wait()
        far_value = dot_nt(far, w_both_t_ref[width:]).astype(LOW)
        value_ref[here] = far_value
        value_t_ref[:, here] = far_value.T
        feats_t_ref[:, here] = far.T
    for copy in head_needs:
        copy.wait()
    span = group * head_size
    row = lax.broadcasted_iota(jnp.int32, (span, block), 0) // head_size
    col = lax.broadcasted_iota(jnp.int32, (block, span), 1) // head_size
    for batch in range(0, heads, together):
        batch_heads = range(batch, batch + together)
        deltas = {}

        def places(head):
            first = head - head % group
            cols = slice(first * head_size, first * head_size + span)
            rows = slice(head * head_size, (head + 1) * head_size)
            lanes = slice((head - batch) * block, (head - batch + 1) * block)
            return head % group, cols, rows, lanes

        for head in batch_heads:
            inner, cols, rows, lanes = places(head)
            shift = lse_ref[head : head + 1, :] * log2e
            query_t = query_t_ref[cols, :]
            query_one = jnp.where(row == inner, query_t, jnp.zeros_like(query_t))
            for start in range(0, members, chunk):
                here = slice(start, start + chunk)
                score = dot(key_ref[here, cols], query_one)
                prob = jnp.exp2(jnp.minimum(score * (scaling * log2e) - shift, 0.0))
                prob_ref[here, lanes] = prob.astype(LOW)
        for head in batch_heads:
            inner, cols, rows, lanes = places(head)
            out_t = dot(value_t_ref[rows, :], prob_ref[:, lanes]).astype(LOW)
            out_t_ref[rows, :] = out_t
            d_rows = d_out_t_ref[rows, :].astype(WIDE)
            deltas[head] = jnp.sum(d_rows * out_t.astype(WIDE), axis=0, keepdims=True) * scaling
        for head in batch_heads:
            inner, cols, rows, lanes = places(head)
            d_out_t = d_out_t_ref[cols, :] * scaling
            d_out_one = jnp.where(row == inner, d_out_t, jnp.zeros_like(d_out_t))
            for start in range(0, members, chunk):
                here = slice(start, start + chunk)
                grad_prob = dot(value_ref[here, cols], d_out_one)
                grad_score = prob_ref[here, lanes].astype(WIDE) * (grad_prob - deltas[head])
                grad_score_ref[here, lanes] = grad_score.astype(LOW)
        for first in range(batch, batch + together, group):
            _, cols, _, _ = places(first)
            later = slice(width + cols.start, width + cols.stop)
            lanes = slice((first - batch) * block, (first - batch + group) * block)
            query, d_out = query_ref[:, cols], d_out_ref[:, cols]
            queries = [jnp.where(col == inner, query, jnp.zeros_like(query)) for inner in range(group)]
            d_outs = [jnp.where(col == inner, d_out, jnp.zeros_like(d_out)) for inner in range(group)]
            queries, d_outs = jnp.concatenate(queries, axis=0), jnp.concatenate(d_outs, axis=0)
            for start in range(0, members, chunk):
                here = slice(start, start + chunk)
                grad_both_ref[here, cols] = dot(grad_score_ref[here, lanes], queries).astype(LOW)
                grad_both_ref[here, later] = dot(prob_ref[here, lanes], d_outs).astype(LOW)
        for head in batch_heads:
            inner, cols, rows, lanes = places(head)
            grad_query_t_ref[rows, :] = dot(key_t_ref[rows, :], grad_score_ref[:, lanes]).astype(LOW)
    for copy in last_needs:
        copy.wait()

    _, tall, wide = keep_ref.shape
    n_outer = width // tall
    me = me_ref[0]
    odd = me % 2 == 1

    def place(start, total):
        low = total.astype(LOW)
        for offset in range(0, total.shape[1], 2 * wide):
            inner = (start + offset) // wide
            for outer in range(n_outer):
                differ = me ^ (outer * n_inner + inner)
                slot = 0
                for masks in stages:
                    for mask in masks:
                        slot = slot * 2 + jnp.where((differ & mask) != 0, 1, 0)
                here = slice(outer * tall, (outer + 1) * tall)
                left = low[here, offset : offset + wide]
                right = low[here, offset + wide : offset + 2 * wide]
                keep_ref[slot] = jnp.where(odd, right, left)
                send_ref[slot] = jnp.where(odd, left, right)

    place(3 * width, dot(out_t_ref[...], grad_out_ref[...]))
    place(0, dot_nt(feats_t_ref[:, :block], grad_query_t_ref[...]))
    for start in range(0, 2 * width, block):
        place(width + start, dot(feats_t_ref[...], grad_both_ref[:, start : start + block]))
    store(send_ref, send_hbm)
    store(keep_ref, keep_hbm)
    for member in range(4):
        here = slice(member * block, (member + 1) * block)
        total = dot(grad_both_ref[here], w_both_t_ref[...])
        if member == 0:
            own_ref[...] = total + lax.dot_general(
                grad_query_t_ref[...],
                w_query_t_ref[...],
                (((0,), (0,)), ((), ())),
                preferred_element_type=WIDE,
            )
            store(own_ref, own_hbm)
        else:
            terms_ref[member - 1] = total.astype(LOW).reshape(terms_ref.shape[1:])
            store(terms_ref.at[member - 1], by_match(terms_hbm, member - 1))
    for copy in stores:
        copy.wait()


def attention(me, stages, arrived, packed, block, width, log_sum_exp):
    n_outer, n_inner = lax.axis_size("gx"), lax.axis_size("gy")
    heads = log_sum_exp.shape[0]
    head_size = width // heads
    members = 4 * block
    group = max(1, 128 // head_size)
    together = min(heads, group)
    devices, _, piece, _ = arrived.shape
    whole_tiles = piece % 8 == 0
    if not whole_tiles:
        arrived = arrived.transpose(1, 0, 2, 3).reshape(3, block, width)
    staged = (3, devices, piece, width) if whole_tiles else (3, block, width)
    half = (devices // 2, width // n_outer, 4 * width // n_inner)
    plain, turned, square = (
        pltpu.VMEM((block, width), LOW),
        pltpu.VMEM((width, block), LOW),
        pltpu.VMEM((width, width), LOW),
    )
    long, long_t = pltpu.VMEM((members, width), LOW), pltpu.VMEM((width, members), LOW)
    terms, own, keep, send = pl.pallas_call(
        functools.partial(attention_kernel, head_size, group, together, 2 * block, stages, n_inner),
        out_shape=(shaped(arrived.shape), shaped((block, width), WIDE), shaped(half), shaped(half)),
        in_specs=[pl.BlockSpec(memory_space=pltpu.SMEM), ANY, VMEM, ANY],
        out_specs=(ANY,) * 4,
        scratch_shapes=[
            plain,
            turned,
            plain,
            turned,
            square,
            pltpu.VMEM((2 * width, width), LOW),
            long_t,
            plain,
            long,
            long,
            long_t,
            long_t,
            pltpu.VMEM(staged, LOW),
            pltpu.VMEM((block, width), WIDE),
            turned,
            turned,
            pltpu.VMEM((members, 2 * width), LOW),
            pltpu.VMEM(half, LOW),
            pltpu.VMEM(half, LOW),
            pltpu.VMEM((members, together * block), LOW),
            pltpu.VMEM((members, together * block), LOW),
            pltpu.VMEM((heads, block), WIDE),
            pltpu.SemaphoreType.DMA((17,)),
            pltpu.SemaphoreType.DMA((6,)),
        ],
        compiler_params=pltpu.CompilerParams(vmem_limit_bytes=MOST_VMEM),
        cost_estimate=pl.CostEstimate(
            flops=12 * block * members * width + 32 * members * width * width,
            bytes_accessed=16 * members * width,
            transcendentals=heads * block * members,
        ),
    )(me.reshape(1), log_sum_exp, arrived, packed)
    if not whole_tiles:
        terms = terms.reshape(3, devices, piece, width).transpose(1, 0, 2, 3)
    return terms, own, keep, send


def bits_of(count):
    return [1 << position for position in range(count.bit_length() - 1)]


def stages_of(n_outer, n_inner):
    outer = [mask * n_inner for mask in bits_of(n_outer)]
    inner = bits_of(n_inner)[1:]
    order = []
    for position in range(max(len(outer), len(inner))):
        order += inner[position : position + 1] + outer[position : position + 1]
    return [order[start : start + 2] for start in range(0, len(order), 2)]


def add_up(first, *others):
    total = first.astype(WIDE)
    for other in others:
        total = total + other.astype(WIDE)
    return total


def swap(value, mask, devices):
    return lax.ppermute(value, AXES, [(device, device ^ mask) for device in range(devices)])


def stage_sum(parts, masks, devices):
    got = []
    for index in range(1, len(parts)):
        mask = 0
        for position, each in enumerate(masks):
            if index >> (len(masks) - 1 - position) & 1:
                mask |= each
        got.append(swap(parts[index], mask, devices))
    return parts[0], got


def collect_kernel(partners_ref, returned_ref, summed_ref):
    for node in range(summed_ref.shape[0]):
        total = None
        for match in range(3):
            term = returned_ref[partners_ref[node, match], match].astype(WIDE)
            total = term if total is None else total + term
        summed_ref[node] = total.astype(LOW)


def collect_pieces(returned, partners):
    devices, _, piece, width = returned.shape
    if piece % 8:
        return sum(returned[partners[:, match], match].astype(WIDE) for match in range(3)).astype(LOW)
    return pl.pallas_call(
        collect_kernel,
        out_shape=shaped((devices, piece, width)),
        in_specs=[pl.BlockSpec(memory_space=pltpu.SMEM), VMEM],
        out_specs=VMEM,
        compiler_params=pltpu.CompilerParams(vmem_limit_bytes=LITTLE_VMEM),
    )(partners, returned)


def finish_kernel(own_ref, back_ref, keep_ref, *refs):
    *got_refs, nodes_ref, weights_ref = refs
    back = back_ref[...].reshape(own_ref.shape)
    nodes_ref[...] = (own_ref[...] + back.astype(WIDE)).astype(LOW)
    weights_ref[...] = add_up(keep_ref[0], *(each[0] for each in got_refs))


def finish(own, back, keep, got):
    _, tall, wide = keep.shape
    return pl.pallas_call(
        finish_kernel,
        out_shape=(shaped(own.shape), shaped((tall, wide), WIDE)),
        in_specs=[VMEM] * (3 + len(got)),
        out_specs=(VMEM, VMEM),
        compiler_params=pltpu.CompilerParams(vmem_limit_bytes=LITTLE_VMEM),
    )(own, back, keep, *got)


def on_device(node_feats, grad_out, log_sum_exp, w_query, w_key, w_value, w_output, partners):
    block, width = node_feats.shape
    n_outer, n_inner = lax.axis_size("gx"), lax.axis_size("gy")
    devices = n_outer * n_inner
    piece = block // devices
    me = lax.axis_index("gx") * n_inner + lax.axis_index("gy")
    stages = stages_of(n_outer, n_inner)

    spread = exchange(node_feats.reshape(devices, piece, width))
    arrived = exchange(spread[partners])
    packed = project(node_feats, grad_out, w_query, w_key, w_value, w_output)
    terms, own, keep, send = attention(me, stages, arrived, packed, block, width, log_sum_exp)
    returned = exchange(terms)
    got = [swap(send, 1, devices)]
    summed = collect_pieces(returned, partners)
    for number, masks in enumerate(stages):
        count = 2 ** len(masks)
        if number == 1:
            keep, _ = lax.optimization_barrier((keep, summed))
        keep = keep.reshape((count, -1) + keep.shape[1:])
        got = [each.reshape(keep.shape) for each in got]
        parts = [
            add_up(keep[index], *(each[index] for each in got)).astype(LOW) for index in range(count)
        ]
        keep, got = stage_sum(parts, masks, devices)
    back = exchange(summed)
    if piece % 8:
        back = back.reshape(block, width)
    grad_nodes, weight_grads = finish(own, back, keep, got)
    return grad_nodes, weight_grads


def solution(mesh):
    return jax.shard_map(
        on_device,
        mesh=mesh,
        in_specs=(
            P(AXES, None),
            P(AXES, None),
            P(None, AXES),
            P(),
            P(),
            P(),
            P(),
            P(),
        ),
        out_specs=(P(AXES, None), P("gx", "gy")),
        check_vma=False,
    )
```

```python
import functools
import math

import jax
import jax.numpy as jnp
from jax import lax
from jax.experimental import pallas as pl
from jax.experimental.pallas import tpu as pltpu
from jax.sharding import PartitionSpec as P

AXES = ("gx", "gy")
LOW = jnp.bfloat16
WIDE = jnp.float32


def dot(left, right):
    return jnp.dot(left, right, preferred_element_type=WIDE)


def dot_nt(left, right):
    return lax.dot_general(left, right, (((1,), (1,)), ((), ())), preferred_element_type=WIDE)


def exchange(pieces):
    return lax.all_to_all(pieces, AXES, split_axis=0, concat_axis=0, tiled=True)


VMEM = pl.BlockSpec(memory_space=pltpu.VMEM)
ANY = pl.BlockSpec(memory_space=pl.ANY)
FULL_VMEM = 56 * 1024 * 1024
MOST_VMEM = 50 * 1024 * 1024
LITTLE_VMEM = 8 * 1024 * 1024


def shaped(shape, dtype=LOW):
    return jax.ShapeDtypeStruct(shape, dtype)


def packing(block, width):
    rows, places = 0, {}
    for name in ("w_key_t", "w_value_t", "w_query_t"):
        places[name] = (pl.ds(rows, width), pl.ds(0, width))
        rows += width
    for name in ("query", "d_out", "key", "value", "grad_out"):
        places[name] = (pl.ds(rows, block), pl.ds(0, width))
        rows += block
    for pair in (("query_t", "d_out_t"), ("key_t", "value_t"), ("feats_t",)):
        for position, name in enumerate(pair):
            places[name] = (pl.ds(rows, width), pl.ds(position * block, block))
        rows += width
    return rows, places


def project_kernel(
    feats_ref, grad_out_ref, w_query_ref, w_key_ref, w_value_ref, w_output_ref, packed_ref
):
    block, width = feats_ref.shape
    _, places = packing(block, width)

    def put(name, value):
        packed_ref[places[name]] = value.astype(LOW)

    feats = feats_ref[...]
    grad_out = grad_out_ref[...]
    put("feats_t", feats.T)
    put("grad_out", grad_out)
    for name, w_ref in (("query", w_query_ref), ("key", w_key_ref), ("value", w_value_ref)):
        put("w_" + name + "_t", w_ref[...].T)
        projected = dot(feats, w_ref[...]).astype(LOW)
        put(name, projected)
        put(name + "_t", projected.T)
    d_out = dot_nt(grad_out, w_output_ref[...]).astype(LOW)
    put("d_out", d_out)
    put("d_out_t", d_out.T)


def project(node_feats, grad_out, *weights):
    block, width = node_feats.shape
    rows, _ = packing(block, width)
    return pl.pallas_call(
        project_kernel,
        out_shape=shaped((rows, width)),
        in_specs=[VMEM] * 6,
        out_specs=VMEM,
        compiler_params=pltpu.CompilerParams(vmem_limit_bytes=FULL_VMEM),
        cost_estimate=pl.CostEstimate(
            flops=8 * block * width * width,
            bytes_accessed=2 * (10 * block * width + 7 * width * width),
            transcendentals=0,
        ),
    )(node_feats, grad_out, *weights)


def attention_kernel(
    head_size,
    group,
    together,
    chunk,
    stages,
    n_inner,
    me_ref,
    lse_hbm,
    arrived_ref,
    packed_hbm,
    terms_hbm,
    own_both_hbm,
    grad_query_t_hbm,
    keep_hbm,
    send_hbm,
    query_ref,
    query_t_ref,
    d_out_ref,
    d_out_t_ref,
    w_both_t_ref,
    feats_t_ref,
    grad_out_ref,
    key_ref,
    value_ref,
    key_t_ref,
    value_t_ref,
    terms_ref,
    grad_query_t_ref,
    out_t_ref,
    grad_both_ref,
    keep_ref,
    send_ref,
    prob_ref,
    grad_score_ref,
    lse_ref,
    in_sem,
    out_sem,
):
    heads = lse_ref.shape[0]
    block, width = query_ref.shape
    members = 4 * block
    scaling = head_size ** (-0.5)
    log2e = math.log2(math.e)

    def by_match(ref, match):
        return ref.at[:, match] if len(ref.shape) == 4 else ref.at[match]

    loads = []

    def load(source, target):
        copy = pltpu.make_async_copy(source, target, in_sem.at[len(loads)])
        copy.start()
        loads.append(copy)
        return copy

    stores = []

    def store(source, target):
        copy = pltpu.make_async_copy(source, target, out_sem.at[len(stores)])
        copy.start()
        stores.append(copy)

    _, places = packing(block, width)

    def part(name):
        return packed_hbm.at[places[name]]

    def far_rows(match):
        rows = arrived_ref[:, match] if len(arrived_ref.shape) == 4 else arrived_ref[match]
        return rows.reshape(block, width)

    own = pl.ds(0, block)
    key_need = load(part("w_key_t"), w_both_t_ref.at[pl.ds(0, width)])
    value_need = load(part("w_value_t"), w_both_t_ref.at[pl.ds(width, width)])
    head_needs = [
        load(lse_hbm, lse_ref),
        load(part("key"), key_ref.at[own]),
        load(part("query_t"), query_t_ref),
        load(part("value_t"), value_t_ref.at[:, own]),
        load(part("value"), value_ref.at[own]),
        load(part("d_out_t"), d_out_t_ref),
        load(part("key_t"), key_t_ref.at[:, own]),
        load(part("query"), query_ref),
        load(part("d_out"), d_out_ref),
    ]
    last_needs = [
        load(part("feats_t"), feats_t_ref.at[:, own]),
        load(part("grad_out"), grad_out_ref),
    ]
    key_need.wait()
    for match in range(3):
        here = slice((match + 1) * block, (match + 2) * block)
        far = far_rows(match)
        far_key = dot_nt(far, w_both_t_ref[:width]).astype(LOW)
        key_ref[here] = far_key
        key_t_ref[:, here] = far_key.T
        if match == 0:
            value_need.wait()
        far_value = dot_nt(far, w_both_t_ref[width:]).astype(LOW)
        value_ref[here] = far_value
        value_t_ref[:, here] = far_value.T
        feats_t_ref[:, here] = far.T
    for copy in head_needs:
        copy.wait()
    span = group * head_size
    row = lax.broadcasted_iota(jnp.int32, (span, block), 0) // head_size
    col = lax.broadcasted_iota(jnp.int32, (block, span), 1) // head_size
    for batch in range(0, heads, together):
        batch_heads = range(batch, batch + together)
        deltas = {}

        def places(head):
            first = head - head % group
            cols = slice(first * head_size, first * head_size + span)
            rows = slice(head * head_size, (head + 1) * head_size)
            lanes = slice((head - batch) * block, (head - batch + 1) * block)
            return head % group, cols, rows, lanes

        for head in batch_heads:
            inner, cols, rows, lanes = places(head)
            shift = lse_ref[head : head + 1, :] * log2e
            query_t = query_t_ref[cols, :]
            query_one = jnp.where(row == inner, query_t, jnp.zeros_like(query_t))
            for start in range(0, members, chunk):
                here = slice(start, start + chunk)
                score = dot(key_ref[here, cols], query_one)
                prob = jnp.exp2(jnp.minimum(score * (scaling * log2e) - shift, 0.0))
                prob_ref[here, lanes] = prob.astype(LOW)
        for head in batch_heads:
            inner, cols, rows, lanes = places(head)
            out_t = dot(value_t_ref[rows, :], prob_ref[:, lanes]).astype(LOW)
            out_t_ref[rows, :] = out_t
            d_rows = d_out_t_ref[rows, :].astype(WIDE)
            deltas[head] = jnp.sum(d_rows * out_t.astype(WIDE), axis=0, keepdims=True) * scaling
        for head in batch_heads:
            inner, cols, rows, lanes = places(head)
            d_out_t = d_out_t_ref[cols, :] * scaling
            d_out_one = jnp.where(row == inner, d_out_t, jnp.zeros_like(d_out_t))
            for start in range(0, members, chunk):
                here = slice(start, start + chunk)
                grad_prob = dot(value_ref[here, cols], d_out_one)
                grad_score = prob_ref[here, lanes].astype(WIDE) * (grad_prob - deltas[head])
                grad_score_ref[here, lanes] = grad_score.astype(LOW)
        for first in range(batch, batch + together, group):
            _, cols, _, _ = places(first)
            later = slice(width + cols.start, width + cols.stop)
            lanes = slice((first - batch) * block, (first - batch + group) * block)
            query, d_out = query_ref[:, cols], d_out_ref[:, cols]
            queries = [jnp.where(col == inner, query, jnp.zeros_like(query)) for inner in range(group)]
            d_outs = [jnp.where(col == inner, d_out, jnp.zeros_like(d_out)) for inner in range(group)]
            queries, d_outs = jnp.concatenate(queries, axis=0), jnp.concatenate(d_outs, axis=0)
            for start in range(0, members, chunk):
                here = slice(start, start + chunk)
                grad_both_ref[here, cols] = dot(grad_score_ref[here, lanes], queries).astype(LOW)
                grad_both_ref[here, later] = dot(prob_ref[here, lanes], d_outs).astype(LOW)
        for head in batch_heads:
            inner, cols, rows, lanes = places(head)
            grad_query_t_ref[rows, :] = dot(key_t_ref[rows, :], grad_score_ref[:, lanes]).astype(LOW)
    for copy in last_needs:
        copy.wait()

    _, tall, wide = keep_ref.shape
    n_outer = width // tall
    me = me_ref[0]
    odd = me % 2 == 1

    def place(start, total):
        low = total.astype(LOW)
        for offset in range(0, total.shape[1], 2 * wide):
            inner = (start + offset) // wide
            for outer in range(n_outer):
                differ = me ^ (outer * n_inner + inner)
                slot = 0
                for masks in stages:
                    for mask in masks:
                        slot = slot * 2 + jnp.where((differ & mask) != 0, 1, 0)
                here = slice(outer * tall, (outer + 1) * tall)
                left = low[here, offset : offset + wide]
                right = low[here, offset + wide : offset + 2 * wide]
                keep_ref[slot] = jnp.where(odd, right, left)
                send_ref[slot] = jnp.where(odd, left, right)

    place(3 * width, dot(out_t_ref[...], grad_out_ref[...]))
    place(0, dot_nt(feats_t_ref[:, :block], grad_query_t_ref[...]))
    for start in range(0, 2 * width, 2 * block):
        place(width + start, dot(feats_t_ref[...], grad_both_ref[:, start : start + 2 * block]))
    store(send_ref, send_hbm)
    store(keep_ref, keep_hbm)
    store(grad_both_ref.at[own], own_both_hbm)
    store(grad_query_t_ref, grad_query_t_hbm)
    for match in range(3):
        here = slice((match + 1) * block, (match + 2) * block)
        total = dot(grad_both_ref[here], w_both_t_ref[...])
        terms_ref[match] = total.astype(LOW).reshape(terms_ref.shape[1:])
        store(terms_ref.at[match], by_match(terms_hbm, match))
    for copy in stores:
        copy.wait()


def attention(me, stages, arrived, packed, block, width, log_sum_exp):
    n_outer, n_inner = lax.axis_size("gx"), lax.axis_size("gy")
    heads = log_sum_exp.shape[0]
    head_size = width // heads
    members = 4 * block
    group = max(1, 128 // head_size)
    together = min(heads, group)
    devices, _, piece, _ = arrived.shape
    whole_tiles = piece % 8 == 0
    if not whole_tiles:
        arrived = arrived.transpose(1, 0, 2, 3).reshape(3, block, width)
    staged = (3, devices, piece, width) if whole_tiles else (3, block, width)
    half = (devices // 2, width // n_outer, 4 * width // n_inner)
    plain, turned = (
        pltpu.VMEM((block, width), LOW),
        pltpu.VMEM((width, block), LOW),
    )
    long, long_t = pltpu.VMEM((members, width), LOW), pltpu.VMEM((width, members), LOW)
    terms, own_both, grad_query_t, keep, send = pl.pallas_call(
        functools.partial(attention_kernel, head_size, group, together, 2 * block, stages, n_inner),
        out_shape=(
            shaped(arrived.shape),
            shaped((block, 2 * width)),
            shaped((width, block)),
            shaped(half),
            shaped(half),
        ),
        in_specs=[pl.BlockSpec(memory_space=pltpu.SMEM), ANY, VMEM, ANY],
        out_specs=(ANY,) * 5,
        scratch_shapes=[
            plain,
            turned,
            plain,
            turned,
            pltpu.VMEM((2 * width, width), LOW),
            long_t,
            plain,
            long,
            long,
            long_t,
            long_t,
            pltpu.VMEM(staged, LOW),
            turned,
            turned,
            pltpu.VMEM((members, 2 * width), LOW),
            pltpu.VMEM(half, LOW),
            pltpu.VMEM(half, LOW),
            pltpu.VMEM((members, together * block), LOW),
            pltpu.VMEM((members, together * block), LOW),
            pltpu.VMEM((heads, block), WIDE),
            pltpu.SemaphoreType.DMA((17,)),
            pltpu.SemaphoreType.DMA((8,)),
        ],
        compiler_params=pltpu.CompilerParams(vmem_limit_bytes=MOST_VMEM),
        cost_estimate=pl.CostEstimate(
            flops=12 * block * members * width + 32 * members * width * width,
            bytes_accessed=16 * members * width,
            transcendentals=heads * block * members,
        ),
    )(me.reshape(1), log_sum_exp, arrived, packed)
    if not whole_tiles:
        terms = terms.reshape(3, devices, piece, width).transpose(1, 0, 2, 3)
    return terms, own_both, grad_query_t, keep, send


def own_kernel(both_ref, grad_query_t_ref, packed_hbm, own_ref, weights_ref, sem):
    width, block = grad_query_t_ref.shape
    _, places = packing(block, width)
    copies = []
    for number, name in enumerate(("w_key_t", "w_value_t", "w_query_t")):
        target = weights_ref.at[pl.ds(number * width, width)]
        copies.append(pltpu.make_async_copy(packed_hbm.at[places[name]], target, sem.at[number]))
        copies[-1].start()
    for copy in copies:
        copy.wait()
    total = dot(both_ref[...], weights_ref[: 2 * width])
    own_ref[...] = total + dot(grad_query_t_ref[...].T, weights_ref[2 * width :])


def own_terms(own_both, grad_query_t, packed):
    width, block = grad_query_t.shape
    return pl.pallas_call(
        own_kernel,
        out_shape=shaped((block, width), WIDE),
        in_specs=[VMEM, VMEM, ANY],
        out_specs=VMEM,
        scratch_shapes=[pltpu.VMEM((3 * width, width), LOW), pltpu.SemaphoreType.DMA((3,))],
        compiler_params=pltpu.CompilerParams(vmem_limit_bytes=MOST_VMEM),
        cost_estimate=pl.CostEstimate(
            flops=6 * block * width * width,
            bytes_accessed=2 * (5 * block * width + 3 * width * width),
            transcendentals=0,
        ),
    )(own_both, grad_query_t, packed)


def bits_of(count):
    return [1 << position for position in range(count.bit_length() - 1)]


def stages_of(n_outer, n_inner):
    outer = [mask * n_inner for mask in bits_of(n_outer)]
    inner = bits_of(n_inner)[1:]
    order = []
    for position in range(max(len(outer), len(inner))):
        order += inner[position : position + 1] + outer[position : position + 1]
    return [order[start : start + 2] for start in range(0, len(order), 2)]


def add_up(first, *others):
    total = first.astype(WIDE)
    for other in others:
        total = total + other.astype(WIDE)
    return total


def swap(value, mask, devices):
    return lax.ppermute(value, AXES, [(device, device ^ mask) for device in range(devices)])


def stage_sum(parts, masks, devices):
    got = []
    for index in range(1, len(parts)):
        mask = 0
        for position, each in enumerate(masks):
            if index >> (len(masks) - 1 - position) & 1:
                mask |= each
        got.append(swap(parts[index], mask, devices))
    return parts[0], got


def collect_kernel(partners_ref, returned_ref, summed_ref):
    for node in range(summed_ref.shape[0]):
        total = None
        for match in range(3):
            term = returned_ref[partners_ref[node, match], match].astype(WIDE)
            total = term if total is None else total + term
        summed_ref[node] = total.astype(LOW)


def collect_pieces(returned, partners):
    devices, _, piece, width = returned.shape
    if piece % 8:
        return sum(returned[partners[:, match], match].astype(WIDE) for match in range(3)).astype(LOW)
    return pl.pallas_call(
        collect_kernel,
        out_shape=shaped((devices, piece, width)),
        in_specs=[pl.BlockSpec(memory_space=pltpu.SMEM), VMEM],
        out_specs=VMEM,
        compiler_params=pltpu.CompilerParams(vmem_limit_bytes=LITTLE_VMEM),
    )(partners, returned)


def finish_kernel(own_ref, back_ref, keep_ref, *refs):
    *got_refs, nodes_ref, weights_ref = refs
    back = back_ref[...].reshape(own_ref.shape)
    nodes_ref[...] = (own_ref[...] + back.astype(WIDE)).astype(LOW)
    weights_ref[...] = add_up(keep_ref[0], *(each[0] for each in got_refs))


def finish(own, back, keep, got):
    _, tall, wide = keep.shape
    return pl.pallas_call(
        finish_kernel,
        out_shape=(shaped(own.shape), shaped((tall, wide), WIDE)),
        in_specs=[VMEM] * (3 + len(got)),
        out_specs=(VMEM, VMEM),
        compiler_params=pltpu.CompilerParams(vmem_limit_bytes=LITTLE_VMEM),
    )(own, back, keep, *got)


def on_device(node_feats, grad_out, log_sum_exp, w_query, w_key, w_value, w_output, partners):
    block, width = node_feats.shape
    n_outer, n_inner = lax.axis_size("gx"), lax.axis_size("gy")
    devices = n_outer * n_inner
    piece = block // devices
    me = lax.axis_index("gx") * n_inner + lax.axis_index("gy")
    stages = stages_of(n_outer, n_inner)

    spread = exchange(node_feats.reshape(devices, piece, width))
    arrived = exchange(spread[partners])
    packed = project(node_feats, grad_out, w_query, w_key, w_value, w_output)
    terms, own_both, grad_query_t, keep, send = attention(
        me, stages, arrived, packed, block, width, log_sum_exp
    )
    own = own_terms(own_both, grad_query_t, packed)
    returned = exchange(terms)
    got = [swap(send, 1, devices)]
    summed = collect_pieces(returned, partners)
    for number, masks in enumerate(stages):
        count = 2 ** len(masks)
        if number == 1:
            keep, _ = lax.optimization_barrier((keep, summed))
        keep = keep.reshape((count, -1) + keep.shape[1:])
        got = [each.reshape(keep.shape) for each in got]
        parts = [
            add_up(keep[index], *(each[index] for each in got)).astype(LOW) for index in range(count)
        ]
        keep, got = stage_sum(parts, masks, devices)
    back = exchange(summed)
    if piece % 8:
        back = back.reshape(block, width)
    grad_nodes, weight_grads = finish(own, back, keep, got)
    return grad_nodes, weight_grads


def solution(mesh):
    return jax.shard_map(
        on_device,
        mesh=mesh,
        in_specs=(
            P(AXES, None),
            P(AXES, None),
            P(None, AXES),
            P(),
            P(),
            P(),
            P(),
            P(),
        ),
        out_specs=(P(AXES, None), P("gx", "gy")),
        check_vma=False,
    )
```

```python
import functools
import math

import jax
import jax.numpy as jnp
from jax import lax
from jax.experimental import pallas as pl
from jax.experimental.pallas import tpu as pltpu
from jax.sharding import PartitionSpec as P

AXES = ("gx", "gy")
LOW = jnp.bfloat16
WIDE = jnp.float32


def dot(left, right):
    return jnp.dot(left, right, preferred_element_type=WIDE)


def dot_nt(left, right):
    return lax.dot_general(left, right, (((1,), (1,)), ((), ())), preferred_element_type=WIDE)


def exchange(pieces):
    return lax.all_to_all(pieces, AXES, split_axis=0, concat_axis=0, tiled=True)


VMEM = pl.BlockSpec(memory_space=pltpu.VMEM)
ANY = pl.BlockSpec(memory_space=pl.ANY)
FULL_VMEM = 56 * 1024 * 1024
MOST_VMEM = 50 * 1024 * 1024
LITTLE_VMEM = 8 * 1024 * 1024


def shaped(shape, dtype=LOW):
    return jax.ShapeDtypeStruct(shape, dtype)


def packing(block, width):
    rows, places = 0, {}
    for name in ("w_key_t", "w_value_t", "w_query_t"):
        places[name] = (pl.ds(rows, width), pl.ds(0, width))
        rows += width
    for name in ("query", "d_out", "key", "value", "grad_out"):
        places[name] = (pl.ds(rows, block), pl.ds(0, width))
        rows += block
    for pair in (("query_t", "d_out_t"), ("key_t", "value_t"), ("feats_t",)):
        for position, name in enumerate(pair):
            places[name] = (pl.ds(rows, width), pl.ds(position * block, block))
        rows += width
    return rows, places


def project_kernel(
    feats_ref, grad_out_ref, w_query_ref, w_key_ref, w_value_ref, w_output_ref, packed_ref
):
    block, width = feats_ref.shape
    _, places = packing(block, width)

    def put(name, value):
        packed_ref[places[name]] = value.astype(LOW)

    feats = feats_ref[...]
    grad_out = grad_out_ref[...]
    put("feats_t", feats.T)
    put("grad_out", grad_out)
    for name, w_ref in (("query", w_query_ref), ("key", w_key_ref), ("value", w_value_ref)):
        put("w_" + name + "_t", w_ref[...].T)
        projected = dot(feats, w_ref[...]).astype(LOW)
        put(name, projected)
        put(name + "_t", projected.T)
    d_out = dot_nt(grad_out, w_output_ref[...]).astype(LOW)
    put("d_out", d_out)
    put("d_out_t", d_out.T)


def project(node_feats, grad_out, *weights):
    block, width = node_feats.shape
    rows, _ = packing(block, width)
    return pl.pallas_call(
        project_kernel,
        out_shape=shaped((rows, width)),
        in_specs=[VMEM] * 6,
        out_specs=VMEM,
        compiler_params=pltpu.CompilerParams(vmem_limit_bytes=FULL_VMEM),
        cost_estimate=pl.CostEstimate(
            flops=8 * block * width * width,
            bytes_accessed=2 * (10 * block * width + 7 * width * width),
            transcendentals=0,
        ),
    )(node_feats, grad_out, *weights)


def attention_kernel(
    head_size,
    group,
    together,
    chunk,
    stages,
    n_inner,
    me_ref,
    lse_hbm,
    arrived_ref,
    packed_hbm,
    terms_hbm,
    own_both_hbm,
    grad_query_t_hbm,
    keep_hbm,
    send_hbm,
    query_ref,
    query_t_ref,
    d_out_ref,
    d_out_t_ref,
    w_both_t_ref,
    feats_t_ref,
    grad_out_ref,
    key_ref,
    value_ref,
    key_t_ref,
    value_t_ref,
    terms_ref,
    grad_query_t_ref,
    out_t_ref,
    grad_both_ref,
    keep_ref,
    send_ref,
    prob_ref,
    grad_score_ref,
    lse_ref,
    in_sem,
    out_sem,
):
    heads = lse_ref.shape[0]
    block, width = query_ref.shape
    members = 4 * block
    scaling = head_size ** (-0.5)
    log2e = math.log2(math.e)

    def by_match(ref, match):
        return ref.at[:, match] if len(ref.shape) == 4 else ref.at[match]

    loads = []

    def load(source, target):
        copy = pltpu.make_async_copy(source, target, in_sem.at[len(loads)])
        copy.start()
        loads.append(copy)
        return copy

    stores = []

    def store(source, target):
        copy = pltpu.make_async_copy(source, target, out_sem.at[len(stores)])
        copy.start()
        stores.append(copy)

    _, places = packing(block, width)

    def part(name):
        return packed_hbm.at[places[name]]

    def far_rows(match):
        rows = arrived_ref[:, match] if len(arrived_ref.shape) == 4 else arrived_ref[match]
        return rows.reshape(block, width)

    own = pl.ds(0, block)
    key_need = load(part("w_key_t"), w_both_t_ref.at[pl.ds(0, width)])
    value_need = load(part("w_value_t"), w_both_t_ref.at[pl.ds(width, width)])
    head_needs = [
        load(lse_hbm, lse_ref),
        load(part("key"), key_ref.at[own]),
        load(part("query_t"), query_t_ref),
        load(part("value_t"), value_t_ref.at[:, own]),
        load(part("value"), value_ref.at[own]),
        load(part("d_out_t"), d_out_t_ref),
        load(part("key_t"), key_t_ref.at[:, own]),
        load(part("query"), query_ref),
        load(part("d_out"), d_out_ref),
    ]
    last_needs = [
        load(part("feats_t"), feats_t_ref.at[:, own]),
        load(part("grad_out"), grad_out_ref),
    ]
    for match in range(3):
        feats_t_ref[:, (match + 1) * block : (match + 2) * block] = far_rows(match).T
    key_need.wait()
    for match in range(3):
        here = slice((match + 1) * block, (match + 2) * block)
        far = far_rows(match)
        far_key = dot_nt(far, w_both_t_ref[:width]).astype(LOW)
        key_ref[here] = far_key
        key_t_ref[:, here] = far_key.T
        if match == 0:
            value_need.wait()
        far_value = dot_nt(far, w_both_t_ref[width:]).astype(LOW)
        value_ref[here] = far_value
        value_t_ref[:, here] = far_value.T
    for copy in head_needs:
        copy.wait()
    span = group * head_size
    row = lax.broadcasted_iota(jnp.int32, (span, block), 0) // head_size
    col = lax.broadcasted_iota(jnp.int32, (block, span), 1) // head_size
    for batch in range(0, heads, together):
        batch_heads = range(batch, batch + together)
        deltas = {}

        def places(head):
            first = head - head % group
            cols = slice(first * head_size, first * head_size + span)
            rows = slice(head * head_size, (head + 1) * head_size)
            lanes = slice((head - batch) * block, (head - batch + 1) * block)
            return head % group, cols, rows, lanes

        for head in batch_heads:
            inner, cols, rows, lanes = places(head)
            shift = lse_ref[head : head + 1, :] * log2e
            query_t = query_t_ref[cols, :]
            query_one = jnp.where(row == inner, query_t, jnp.zeros_like(query_t))
            for start in range(0, members, chunk):
                here = slice(start, start + chunk)
                score = dot(key_ref[here, cols], query_one)
                prob = jnp.exp2(jnp.minimum(score * (scaling * log2e) - shift, 0.0))
                prob_ref[here, lanes] = prob.astype(LOW)
        for head in batch_heads:
            inner, cols, rows, lanes = places(head)
            out_t = dot(value_t_ref[rows, :], prob_ref[:, lanes]).astype(LOW)
            out_t_ref[rows, :] = out_t
            d_rows = d_out_t_ref[rows, :].astype(WIDE)
            deltas[head] = jnp.sum(d_rows * out_t.astype(WIDE), axis=0, keepdims=True) * scaling
        for head in batch_heads:
            inner, cols, rows, lanes = places(head)
            d_out_t = d_out_t_ref[cols, :] * scaling
            d_out_one = jnp.where(row == inner, d_out_t, jnp.zeros_like(d_out_t))
            for start in range(0, members, chunk):
                here = slice(start, start + chunk)
                grad_prob = dot(value_ref[here, cols], d_out_one)
                grad_score = prob_ref[here, lanes].astype(WIDE) * (grad_prob - deltas[head])
                grad_score_ref[here, lanes] = grad_score.astype(LOW)
        for first in range(batch, batch + together, group):
            _, cols, _, _ = places(first)
            later = slice(width + cols.start, width + cols.stop)
            lanes = slice((first - batch) * block, (first - batch + group) * block)
            query, d_out = query_ref[:, cols], d_out_ref[:, cols]
            queries = [jnp.where(col == inner, query, jnp.zeros_like(query)) for inner in range(group)]
            d_outs = [jnp.where(col == inner, d_out, jnp.zeros_like(d_out)) for inner in range(group)]
            queries, d_outs = jnp.concatenate(queries, axis=0), jnp.concatenate(d_outs, axis=0)
            for start in range(0, members, chunk):
                here = slice(start, start + chunk)
                grad_both_ref[here, cols] = dot(grad_score_ref[here, lanes], queries).astype(LOW)
                grad_both_ref[here, later] = dot(prob_ref[here, lanes], d_outs).astype(LOW)
        for head in batch_heads:
            inner, cols, rows, lanes = places(head)
            grad_query_t_ref[rows, :] = dot(key_t_ref[rows, :], grad_score_ref[:, lanes]).astype(LOW)
    store(grad_both_ref.at[own], own_both_hbm)
    store(grad_query_t_ref, grad_query_t_hbm)
    for copy in last_needs:
        copy.wait()

    _, tall, wide = keep_ref.shape
    n_outer = width // tall
    me = me_ref[0]
    odd = me % 2 == 1

    def place(start, total):
        low = total.astype(LOW)
        for offset in range(0, total.shape[1], 2 * wide):
            inner = (start + offset) // wide
            for outer in range(n_outer):
                differ = me ^ (outer * n_inner + inner)
                slot = 0
                for masks in stages:
                    for mask in masks:
                        slot = slot * 2 + jnp.where((differ & mask) != 0, 1, 0)
                here = slice(outer * tall, (outer + 1) * tall)
                left = low[here, offset : offset + wide]
                right = low[here, offset + wide : offset + 2 * wide]
                keep_ref[slot] = jnp.where(odd, right, left)
                send_ref[slot] = jnp.where(odd, left, right)

    place(3 * width, dot(out_t_ref[...], grad_out_ref[...]))
    place(0, dot_nt(feats_t_ref[:, :block], grad_query_t_ref[...]))
    for start in range(0, 2 * width, 2 * block):
        place(width + start, dot(feats_t_ref[...], grad_both_ref[:, start : start + 2 * block]))
    store(send_ref, send_hbm)
    store(keep_ref, keep_hbm)
    for match in range(3):
        here = slice((match + 1) * block, (match + 2) * block)
        total = dot(grad_both_ref[here], w_both_t_ref[...])
        terms_ref[match] = total.astype(LOW).reshape(terms_ref.shape[1:])
        store(terms_ref.at[match], by_match(terms_hbm, match))
    for copy in stores:
        copy.wait()


def attention(me, stages, arrived, packed, block, width, log_sum_exp):
    n_outer, n_inner = lax.axis_size("gx"), lax.axis_size("gy")
    heads = log_sum_exp.shape[0]
    head_size = width // heads
    members = 4 * block
    group = max(1, 128 // head_size)
    together = min(heads, group)
    devices, _, piece, _ = arrived.shape
    whole_tiles = piece % 8 == 0
    if not whole_tiles:
        arrived = arrived.transpose(1, 0, 2, 3).reshape(3, block, width)
    staged = (3, devices, piece, width) if whole_tiles else (3, block, width)
    half = (devices // 2, width // n_outer, 4 * width // n_inner)
    plain, turned = (
        pltpu.VMEM((block, width), LOW),
        pltpu.VMEM((width, block), LOW),
    )
    long, long_t = pltpu.VMEM((members, width), LOW), pltpu.VMEM((width, members), LOW)
    terms, own_both, grad_query_t, keep, send = pl.pallas_call(
        functools.partial(attention_kernel, head_size, group, together, 2 * block, stages, n_inner),
        out_shape=(
            shaped(arrived.shape),
            shaped((block, 2 * width)),
            shaped((width, block)),
            shaped(half),
            shaped(half),
        ),
        in_specs=[pl.BlockSpec(memory_space=pltpu.SMEM), ANY, VMEM, ANY],
        out_specs=(ANY,) * 5,
        scratch_shapes=[
            plain,
            turned,
            plain,
            turned,
            pltpu.VMEM((2 * width, width), LOW),
            long_t,
            plain,
            long,
            long,
            long_t,
            long_t,
            pltpu.VMEM(staged, LOW),
            turned,
            turned,
            pltpu.VMEM((members, 2 * width), LOW),
            pltpu.VMEM(half, LOW),
            pltpu.VMEM(half, LOW),
            pltpu.VMEM((members, together * block), LOW),
            pltpu.VMEM((members, together * block), LOW),
            pltpu.VMEM((heads, block), WIDE),
            pltpu.SemaphoreType.DMA((17,)),
            pltpu.SemaphoreType.DMA((8,)),
        ],
        compiler_params=pltpu.CompilerParams(vmem_limit_bytes=MOST_VMEM),
        cost_estimate=pl.CostEstimate(
            flops=12 * block * members * width + 32 * members * width * width,
            bytes_accessed=16 * members * width,
            transcendentals=heads * block * members,
        ),
    )(me.reshape(1), log_sum_exp, arrived, packed)
    if not whole_tiles:
        terms = terms.reshape(3, devices, piece, width).transpose(1, 0, 2, 3)
    return terms, own_both, grad_query_t, keep, send


def own_kernel(both_ref, grad_query_t_ref, packed_hbm, own_ref, weights_ref, sem):
    width, block = grad_query_t_ref.shape
    _, places = packing(block, width)
    copies = []
    for number, name in enumerate(("w_key_t", "w_value_t", "w_query_t")):
        target = weights_ref.at[pl.ds(number * width, width)]
        copies.append(pltpu.make_async_copy(packed_hbm.at[places[name]], target, sem.at[number]))
        copies[-1].start()
    for copy in copies:
        copy.wait()
    total = dot(both_ref[...], weights_ref[: 2 * width])
    own_ref[...] = total + dot(grad_query_t_ref[...].T, weights_ref[2 * width :])


def own_terms(own_both, grad_query_t, packed):
    width, block = grad_query_t.shape
    return pl.pallas_call(
        own_kernel,
        out_shape=shaped((block, width), WIDE),
        in_specs=[VMEM, VMEM, ANY],
        out_specs=VMEM,
        scratch_shapes=[pltpu.VMEM((3 * width, width), LOW), pltpu.SemaphoreType.DMA((3,))],
        compiler_params=pltpu.CompilerParams(vmem_limit_bytes=MOST_VMEM),
        cost_estimate=pl.CostEstimate(
            flops=6 * block * width * width,
            bytes_accessed=2 * (5 * block * width + 3 * width * width),
            transcendentals=0,
        ),
    )(own_both, grad_query_t, packed)


def bits_of(count):
    return [1 << position for position in range(count.bit_length() - 1)]


def stages_of(n_outer, n_inner):
    outer = [mask * n_inner for mask in bits_of(n_outer)]
    inner = bits_of(n_inner)[1:]
    order = []
    for position in range(max(len(outer), len(inner))):
        order += inner[position : position + 1] + outer[position : position + 1]
    return [order[start : start + 2] for start in range(0, len(order), 2)]


def add_up(first, *others):
    total = first.astype(WIDE)
    for other in others:
        total = total + other.astype(WIDE)
    return total


def swap(value, mask, devices):
    return lax.ppermute(value, AXES, [(device, device ^ mask) for device in range(devices)])


def stage_sum(parts, masks, devices):
    got = []
    for index in range(1, len(parts)):
        mask = 0
        for position, each in enumerate(masks):
            if index >> (len(masks) - 1 - position) & 1:
                mask |= each
        got.append(swap(parts[index], mask, devices))
    return parts[0], got


def collect_kernel(partners_ref, returned_ref, summed_ref):
    for node in range(summed_ref.shape[0]):
        total = None
        for match in range(3):
            term = returned_ref[partners_ref[node, match], match].astype(WIDE)
            total = term if total is None else total + term
        summed_ref[node] = total.astype(LOW)


def collect_pieces(returned, partners):
    devices, _, piece, width = returned.shape
    if piece % 8:
        return sum(returned[partners[:, match], match].astype(WIDE) for match in range(3)).astype(LOW)
    return pl.pallas_call(
        collect_kernel,
        out_shape=shaped((devices, piece, width)),
        in_specs=[pl.BlockSpec(memory_space=pltpu.SMEM), VMEM],
        out_specs=VMEM,
        compiler_params=pltpu.CompilerParams(vmem_limit_bytes=LITTLE_VMEM),
    )(partners, returned)


def finish_kernel(own_ref, back_ref, keep_ref, *refs):
    *got_refs, nodes_ref, weights_ref = refs
    back = back_ref[...].reshape(own_ref.shape)
    nodes_ref[...] = (own_ref[...] + back.astype(WIDE)).astype(LOW)
    weights_ref[...] = add_up(keep_ref[0], *(each[0] for each in got_refs))


def finish(own, back, keep, got):
    _, tall, wide = keep.shape
    return pl.pallas_call(
        finish_kernel,
        out_shape=(shaped(own.shape), shaped((tall, wide), WIDE)),
        in_specs=[VMEM] * (3 + len(got)),
        out_specs=(VMEM, VMEM),
        compiler_params=pltpu.CompilerParams(vmem_limit_bytes=LITTLE_VMEM),
    )(own, back, keep, *got)


def on_device(node_feats, grad_out, log_sum_exp, w_query, w_key, w_value, w_output, partners):
    block, width = node_feats.shape
    n_outer, n_inner = lax.axis_size("gx"), lax.axis_size("gy")
    devices = n_outer * n_inner
    piece = block // devices
    me = lax.axis_index("gx") * n_inner + lax.axis_index("gy")
    stages = stages_of(n_outer, n_inner)

    spread = exchange(node_feats.reshape(devices, piece, width))
    arrived = exchange(spread[partners])
    packed = project(node_feats, grad_out, w_query, w_key, w_value, w_output)
    terms, own_both, grad_query_t, keep, send = attention(
        me, stages, arrived, packed, block, width, log_sum_exp
    )
    own = own_terms(own_both, grad_query_t, packed)
    returned = exchange(terms)
    got = [swap(send, 1, devices)]
    summed = collect_pieces(returned, partners)
    for number, masks in enumerate(stages):
        count = 2 ** len(masks)
        if number == 1:
            keep, _ = lax.optimization_barrier((keep, summed))
        keep = keep.reshape((count, -1) + keep.shape[1:])
        got = [each.reshape(keep.shape) for each in got]
        parts = [
            add_up(keep[index], *(each[index] for each in got)).astype(LOW) for index in range(count)
        ]
        keep, got = stage_sum(parts, masks, devices)
    back = exchange(summed)
    if piece % 8:
        back = back.reshape(block, width)
    grad_nodes, weight_grads = finish(own, back, keep, got)
    return grad_nodes, weight_grads


def solution(mesh):
    return jax.shard_map(
        on_device,
        mesh=mesh,
        in_specs=(
            P(AXES, None),
            P(AXES, None),
            P(None, AXES),
            P(),
            P(),
            P(),
            P(),
            P(),
        ),
        out_specs=(P(AXES, None), P("gx", "gy")),
        check_vma=False,
    )
```

```python
import functools
import math

import jax
import jax.numpy as jnp
from jax import lax
from jax.experimental import pallas as pl
from jax.experimental.pallas import tpu as pltpu
from jax.sharding import PartitionSpec as P

AXES = ("gx", "gy")
LOW = jnp.bfloat16
WIDE = jnp.float32


def dot(left, right):
    return jnp.dot(left, right, preferred_element_type=WIDE)


def dot_nt(left, right):
    return lax.dot_general(left, right, (((1,), (1,)), ((), ())), preferred_element_type=WIDE)


def exchange(pieces):
    return lax.all_to_all(pieces, AXES, split_axis=0, concat_axis=0, tiled=True)


VMEM = pl.BlockSpec(memory_space=pltpu.VMEM)
ANY = pl.BlockSpec(memory_space=pl.ANY)
FULL_VMEM = 56 * 1024 * 1024
MOST_VMEM = 50 * 1024 * 1024
LITTLE_VMEM = 8 * 1024 * 1024


def shaped(shape, dtype=LOW):
    return jax.ShapeDtypeStruct(shape, dtype)


def packing(block, width):
    rows, places = 0, {}
    for name in ("w_key_t", "w_value_t", "w_query_t"):
        places[name] = (pl.ds(rows, width), pl.ds(0, width))
        rows += width
    for name in ("query", "d_out", "key", "value", "grad_out"):
        places[name] = (pl.ds(rows, block), pl.ds(0, width))
        rows += block
    for pair in (("query_t", "d_out_t"), ("key_t", "value_t"), ("feats_t",)):
        for position, name in enumerate(pair):
            places[name] = (pl.ds(rows, width), pl.ds(position * block, block))
        rows += width
    return rows, places


def project_kernel(
    feats_ref, grad_out_ref, w_query_ref, w_key_ref, w_value_ref, w_output_ref, packed_ref
):
    block, width = feats_ref.shape
    _, places = packing(block, width)

    def put(name, value):
        packed_ref[places[name]] = value.astype(LOW)

    feats = feats_ref[...]
    grad_out = grad_out_ref[...]
    put("feats_t", feats.T)
    put("grad_out", grad_out)
    for name, w_ref in (("query", w_query_ref), ("key", w_key_ref), ("value", w_value_ref)):
        put("w_" + name + "_t", w_ref[...].T)
        projected = dot(feats, w_ref[...]).astype(LOW)
        put(name, projected)
        put(name + "_t", projected.T)
    d_out = dot_nt(grad_out, w_output_ref[...]).astype(LOW)
    put("d_out", d_out)
    put("d_out_t", d_out.T)


def project(node_feats, grad_out, *weights):
    block, width = node_feats.shape
    rows, _ = packing(block, width)
    return pl.pallas_call(
        project_kernel,
        out_shape=shaped((rows, width)),
        in_specs=[VMEM] * 6,
        out_specs=VMEM,
        compiler_params=pltpu.CompilerParams(vmem_limit_bytes=FULL_VMEM),
        cost_estimate=pl.CostEstimate(
            flops=8 * block * width * width,
            bytes_accessed=2 * (10 * block * width + 7 * width * width),
            transcendentals=0,
        ),
    )(node_feats, grad_out, *weights)


def attention_kernel(
    head_size,
    group,
    together,
    chunk,
    stages,
    n_inner,
    me_ref,
    lse_hbm,
    arrived_ref,
    packed_hbm,
    terms_hbm,
    own_both_hbm,
    grad_query_t_hbm,
    keep_hbm,
    send_hbm,
    query_ref,
    query_t_ref,
    d_out_ref,
    d_out_t_ref,
    w_both_t_ref,
    feats_t_ref,
    grad_out_ref,
    key_ref,
    value_ref,
    key_t_ref,
    value_t_ref,
    terms_ref,
    grad_query_t_ref,
    out_t_ref,
    grad_both_ref,
    keep_ref,
    send_ref,
    prob_ref,
    grad_score_ref,
    lse_ref,
    in_sem,
    out_sem,
):
    heads = lse_ref.shape[0]
    block, width = query_ref.shape
    members = 4 * block
    scaling = head_size ** (-0.5)
    log2e = math.log2(math.e)

    def by_match(ref, match):
        return ref.at[:, match] if len(ref.shape) == 4 else ref.at[match]

    loads = []

    def load(source, target):
        copy = pltpu.make_async_copy(source, target, in_sem.at[len(loads)])
        copy.start()
        loads.append(copy)
        return copy

    stores = []

    def store(source, target):
        copy = pltpu.make_async_copy(source, target, out_sem.at[len(stores)])
        copy.start()
        stores.append(copy)

    _, places = packing(block, width)

    def part(name):
        return packed_hbm.at[places[name]]

    def far_rows(match):
        rows = arrived_ref[:, match] if len(arrived_ref.shape) == 4 else arrived_ref[match]
        return rows.reshape(block, width)

    own = pl.ds(0, block)
    key_need = load(part("w_key_t"), w_both_t_ref.at[pl.ds(0, width)])
    value_need = load(part("w_value_t"), w_both_t_ref.at[pl.ds(width, width)])
    head_needs = [
        load(lse_hbm, lse_ref),
        load(part("key"), key_ref.at[own]),
        load(part("query_t"), query_t_ref),
        load(part("value_t"), value_t_ref.at[:, own]),
        load(part("value"), value_ref.at[own]),
        load(part("d_out_t"), d_out_t_ref),
        load(part("key_t"), key_t_ref.at[:, own]),
        load(part("query"), query_ref),
        load(part("d_out"), d_out_ref),
    ]
    last_needs = [
        load(part("feats_t"), feats_t_ref.at[:, own]),
        load(part("grad_out"), grad_out_ref),
    ]
    for match in range(3):
        feats_t_ref[:, (match + 1) * block : (match + 2) * block] = far_rows(match).T
    key_need.wait()
    for match in range(3):
        here = slice((match + 1) * block, (match + 2) * block)
        far = far_rows(match)
        far_key = dot_nt(far, w_both_t_ref[:width]).astype(LOW)
        key_ref[here] = far_key
        key_t_ref[:, here] = far_key.T
        if match == 0:
            value_need.wait()
        far_value = dot_nt(far, w_both_t_ref[width:]).astype(LOW)
        value_ref[here] = far_value
        value_t_ref[:, here] = far_value.T
    for copy in head_needs:
        copy.wait()
    span = group * head_size
    row = lax.broadcasted_iota(jnp.int32, (span, block), 0) // head_size
    col = lax.broadcasted_iota(jnp.int32, (block, span), 1) // head_size
    for batch in range(0, heads, together):
        batch_heads = range(batch, batch + together)
        deltas = {}

        def places(head):
            first = head - head % group
            cols = slice(first * head_size, first * head_size + span)
            rows = slice(head * head_size, (head + 1) * head_size)
            lanes = slice((head - batch) * block, (head - batch + 1) * block)
            return head % group, cols, rows, lanes

        for head in batch_heads:
            inner, cols, rows, lanes = places(head)
            shift = lse_ref[head : head + 1, :] * log2e
            query_t = query_t_ref[cols, :]
            query_one = jnp.where(row == inner, query_t, jnp.zeros_like(query_t))
            for start in range(0, members, chunk):
                here = slice(start, start + chunk)
                score = dot(key_ref[here, cols], query_one)
                prob = jnp.exp2(jnp.minimum(score * (scaling * log2e) - shift, 0.0))
                prob_ref[here, lanes] = prob.astype(LOW)
        for head in batch_heads:
            inner, cols, rows, lanes = places(head)
            out_t = dot(value_t_ref[rows, :], prob_ref[:, lanes]).astype(LOW)
            out_t_ref[rows, :] = out_t
            d_rows = d_out_t_ref[rows, :].astype(WIDE)
            deltas[head] = jnp.sum(d_rows * out_t.astype(WIDE), axis=0, keepdims=True) * scaling
        for head in batch_heads:
            inner, cols, rows, lanes = places(head)
            d_out_t = d_out_t_ref[cols, :] * scaling
            d_out_one = jnp.where(row == inner, d_out_t, jnp.zeros_like(d_out_t))
            for start in range(0, members, chunk):
                here = slice(start, start + chunk)
                grad_prob = dot(value_ref[here, cols], d_out_one)
                grad_score = prob_ref[here, lanes].astype(WIDE) * (grad_prob - deltas[head])
                grad_score_ref[here, lanes] = grad_score.astype(LOW)
        for first in range(batch, batch + together, group):
            _, cols, _, _ = places(first)
            later = slice(width + cols.start, width + cols.stop)
            lanes = slice((first - batch) * block, (first - batch + group) * block)
            query, d_out = query_ref[:, cols], d_out_ref[:, cols]
            queries = [jnp.where(col == inner, query, jnp.zeros_like(query)) for inner in range(group)]
            d_outs = [jnp.where(col == inner, d_out, jnp.zeros_like(d_out)) for inner in range(group)]
            queries, d_outs = jnp.concatenate(queries, axis=0), jnp.concatenate(d_outs, axis=0)
            for start in range(0, members, chunk):
                here = slice(start, start + chunk)
                grad_both_ref[here, cols] = dot(grad_score_ref[here, lanes], queries).astype(LOW)
                grad_both_ref[here, later] = dot(prob_ref[here, lanes], d_outs).astype(LOW)
        for head in batch_heads:
            inner, cols, rows, lanes = places(head)
            grad_query_t_ref[rows, :] = dot(key_t_ref[rows, :], grad_score_ref[:, lanes]).astype(LOW)
    store(grad_both_ref.at[own], own_both_hbm)
    store(grad_query_t_ref, grad_query_t_hbm)
    for copy in last_needs:
        copy.wait()

    _, tall, wide = keep_ref.shape
    n_outer = width // tall
    me = me_ref[0]
    odd = me % 2 == 1

    def place(start, total):
        low = total.astype(LOW)
        for offset in range(0, total.shape[1], 2 * wide):
            inner = (start + offset) // wide
            for outer in range(n_outer):
                differ = me ^ (outer * n_inner + inner)
                slot = 0
                for masks in stages:
                    for mask in masks:
                        slot = slot * 2 + jnp.where((differ & mask) != 0, 1, 0)
                here = slice(outer * tall, (outer + 1) * tall)
                left = low[here, offset : offset + wide]
                right = low[here, offset + wide : offset + 2 * wide]
                keep_ref[slot] = jnp.where(odd, right, left)
                send_ref[slot] = jnp.where(odd, left, right)

    place(3 * width, dot(out_t_ref[...], grad_out_ref[...]))
    place(0, dot_nt(feats_t_ref[:, :block], grad_query_t_ref[...]))
    for start in range(0, 2 * width, 2 * block):
        place(width + start, dot(feats_t_ref[...], grad_both_ref[:, start : start + 2 * block]))
    store(send_ref, send_hbm)
    store(keep_ref, keep_hbm)
    for match in range(3):
        here = slice((match + 1) * block, (match + 2) * block)
        total = dot(grad_both_ref[here], w_both_t_ref[...])
        terms_ref[match] = total.astype(LOW).reshape(terms_ref.shape[1:])
        store(terms_ref.at[match], by_match(terms_hbm, match))
    for copy in stores:
        copy.wait()


def attention(me, stages, arrived, packed, block, width, log_sum_exp):
    n_outer, n_inner = lax.axis_size("gx"), lax.axis_size("gy")
    heads = log_sum_exp.shape[0]
    head_size = width // heads
    members = 4 * block
    group = max(1, 128 // head_size)
    together = min(heads, group)
    devices, _, piece, _ = arrived.shape
    whole_tiles = piece % 8 == 0
    if not whole_tiles:
        arrived = arrived.transpose(1, 0, 2, 3).reshape(3, block, width)
    staged = (3, devices, piece, width) if whole_tiles else (3, block, width)
    half = (devices // 2, width // n_outer, 4 * width // n_inner)
    plain, turned = (
        pltpu.VMEM((block, width), LOW),
        pltpu.VMEM((width, block), LOW),
    )
    long, long_t = pltpu.VMEM((members, width), LOW), pltpu.VMEM((width, members), LOW)
    terms, own_both, grad_query_t, keep, send = pl.pallas_call(
        functools.partial(attention_kernel, head_size, group, together, block, stages, n_inner),
        out_shape=(
            shaped(arrived.shape),
            shaped((block, 2 * width)),
            shaped((width, block)),
            shaped(half),
            shaped(half),
        ),
        in_specs=[pl.BlockSpec(memory_space=pltpu.SMEM), ANY, VMEM, ANY],
        out_specs=(ANY,) * 5,
        scratch_shapes=[
            plain,
            turned,
            plain,
            turned,
            pltpu.VMEM((2 * width, width), LOW),
            long_t,
            plain,
            long,
            long,
            long_t,
            long_t,
            pltpu.VMEM(staged, LOW),
            turned,
            turned,
            pltpu.VMEM((members, 2 * width), LOW),
            pltpu.VMEM(half, LOW),
            pltpu.VMEM(half, LOW),
            pltpu.VMEM((members, together * block), LOW),
            pltpu.VMEM((members, together * block), LOW),
            pltpu.VMEM((heads, block), WIDE),
            pltpu.SemaphoreType.DMA((17,)),
            pltpu.SemaphoreType.DMA((8,)),
        ],
        compiler_params=pltpu.CompilerParams(vmem_limit_bytes=MOST_VMEM),
        cost_estimate=pl.CostEstimate(
            flops=12 * block * members * width + 32 * members * width * width,
            bytes_accessed=16 * members * width,
            transcendentals=heads * block * members,
        ),
    )(me.reshape(1), log_sum_exp, arrived, packed)
    if not whole_tiles:
        terms = terms.reshape(3, devices, piece, width).transpose(1, 0, 2, 3)
    return terms, own_both, grad_query_t, keep, send


def own_kernel(both_ref, grad_query_t_ref, packed_hbm, own_ref, weights_ref, sem):
    width, block = grad_query_t_ref.shape
    _, places = packing(block, width)
    copies = []
    for number, name in enumerate(("w_key_t", "w_value_t", "w_query_t")):
        target = weights_ref.at[pl.ds(number * width, width)]
        copies.append(pltpu.make_async_copy(packed_hbm.at[places[name]], target, sem.at[number]))
        copies[-1].start()
    for copy in copies:
        copy.wait()
    total = dot(both_ref[...], weights_ref[: 2 * width])
    own_ref[...] = total + dot(grad_query_t_ref[...].T, weights_ref[2 * width :])


def own_terms(own_both, grad_query_t, packed):
    width, block = grad_query_t.shape
    return pl.pallas_call(
        own_kernel,
        out_shape=shaped((block, width), WIDE),
        in_specs=[VMEM, VMEM, ANY],
        out_specs=VMEM,
        scratch_shapes=[pltpu.VMEM((3 * width, width), LOW), pltpu.SemaphoreType.DMA((3,))],
        compiler_params=pltpu.CompilerParams(vmem_limit_bytes=MOST_VMEM),
        cost_estimate=pl.CostEstimate(
            flops=6 * block * width * width,
            bytes_accessed=2 * (5 * block * width + 3 * width * width),
            transcendentals=0,
        ),
    )(own_both, grad_query_t, packed)


def bits_of(count):
    return [1 << position for position in range(count.bit_length() - 1)]


def stages_of(n_outer, n_inner):
    outer = [mask * n_inner for mask in bits_of(n_outer)]
    inner = bits_of(n_inner)[1:]
    order = []
    for position in range(max(len(outer), len(inner))):
        order += inner[position : position + 1] + outer[position : position + 1]
    return [order[start : start + 2] for start in range(0, len(order), 2)]


def add_up(first, *others):
    total = first.astype(WIDE)
    for other in others:
        total = total + other.astype(WIDE)
    return total


def swap(value, mask, devices):
    return lax.ppermute(value, AXES, [(device, device ^ mask) for device in range(devices)])


def stage_sum(parts, masks, devices):
    got = []
    for index in range(1, len(parts)):
        mask = 0
        for position, each in enumerate(masks):
            if index >> (len(masks) - 1 - position) & 1:
                mask |= each
        got.append(swap(parts[index], mask, devices))
    return parts[0], got


def collect_kernel(partners_ref, returned_ref, summed_ref):
    for node in range(summed_ref.shape[0]):
        total = None
        for match in range(3):
            term = returned_ref[partners_ref[node, match], match].astype(WIDE)
            total = term if total is None else total + term
        summed_ref[node] = total.astype(LOW)


def collect_pieces(returned, partners):
    devices, _, piece, width = returned.shape
    if piece % 8:
        return sum(returned[partners[:, match], match].astype(WIDE) for match in range(3)).astype(LOW)
    return pl.pallas_call(
        collect_kernel,
        out_shape=shaped((devices, piece, width)),
        in_specs=[pl.BlockSpec(memory_space=pltpu.SMEM), VMEM],
        out_specs=VMEM,
        compiler_params=pltpu.CompilerParams(vmem_limit_bytes=LITTLE_VMEM),
    )(partners, returned)


def finish_kernel(own_ref, back_ref, keep_ref, *refs):
    *got_refs, nodes_ref, weights_ref = refs
    back = back_ref[...].reshape(own_ref.shape)
    nodes_ref[...] = (own_ref[...] + back.astype(WIDE)).astype(LOW)
    weights_ref[...] = add_up(keep_ref[0], *(each[0] for each in got_refs))


def finish(own, back, keep, got):
    _, tall, wide = keep.shape
    return pl.pallas_call(
        finish_kernel,
        out_shape=(shaped(own.shape), shaped((tall, wide), WIDE)),
        in_specs=[VMEM] * (3 + len(got)),
        out_specs=(VMEM, VMEM),
        compiler_params=pltpu.CompilerParams(vmem_limit_bytes=LITTLE_VMEM),
    )(own, back, keep, *got)


def on_device(node_feats, grad_out, log_sum_exp, w_query, w_key, w_value, w_output, partners):
    block, width = node_feats.shape
    n_outer, n_inner = lax.axis_size("gx"), lax.axis_size("gy")
    devices = n_outer * n_inner
    piece = block // devices
    me = lax.axis_index("gx") * n_inner + lax.axis_index("gy")
    stages = stages_of(n_outer, n_inner)

    spread = exchange(node_feats.reshape(devices, piece, width))
    arrived = exchange(spread[partners])
    packed = project(node_feats, grad_out, w_query, w_key, w_value, w_output)
    terms, own_both, grad_query_t, keep, send = attention(
        me, stages, arrived, packed, block, width, log_sum_exp
    )
    own = own_terms(own_both, grad_query_t, packed)
    returned = exchange(terms)
    got = [swap(send, 1, devices)]
    summed = collect_pieces(returned, partners)
    for number, masks in enumerate(stages):
        count = 2 ** len(masks)
        if number == 1:
            keep, _ = lax.optimization_barrier((keep, summed))
        keep = keep.reshape((count, -1) + keep.shape[1:])
        got = [each.reshape(keep.shape) for each in got]
        parts = [
            add_up(keep[index], *(each[index] for each in got)).astype(LOW) for index in range(count)
        ]
        keep, got = stage_sum(parts, masks, devices)
    back = exchange(summed)
    if piece % 8:
        back = back.reshape(block, width)
    grad_nodes, weight_grads = finish(own, back, keep, got)
    return grad_nodes, weight_grads


def solution(mesh):
    return jax.shard_map(
        on_device,
        mesh=mesh,
        in_specs=(
            P(AXES, None),
            P(AXES, None),
            P(None, AXES),
            P(),
            P(),
            P(),
            P(),
            P(),
        ),
        out_specs=(P(AXES, None), P("gx", "gy")),
        check_vma=False,
    )
```
